32 devices in a mesh: dp: 8 (over y, x, core), tensor: 4 (over z).
Axes of the slice: x: 2, y: 2, z: 4, core: 2. Of those that a mesh axis runs over, the one named last changes fastest.
Arguments:
- tokens: bfloat16 [4096, 768], P(('dp', 'tensor')), may hold values from -6 to 6
- norm_gain_pair: float32 [2, 768], P(None, ('dp', 'tensor')), may hold values from 0.5 to 1.5
- norm_bias_pair: float32 [2, 768], P(None, ('dp', 'tensor')), may hold values from -3 to 3
- w_qkv: bfloat16 [3, 768, 768], P(None, 'dp', 'tensor'), may hold values from -0.21875 to 0.21875
- qv_bias: float32 [2, 768], P(None, ('dp', 'tensor')), may hold values from -3 to 3
- w_out: bfloat16 [768, 768], P('tensor', 'dp'), may hold values from -0.875 to 0.875
- res_bias: float32 [2, 768], P(None, ('dp', 'tensor')), may hold values from -3 to 3
- w_fc: bfloat16 [768, 3072], P('dp', 'tensor'), may hold values from -0.21875 to 0.21875
- fc_bias: float32 [3072], P(('dp', 'tensor')), may hold values from -3 to 3
- w_proj: bfloat16 [3072, 768], P('tensor', 'dp'), may hold values from -0.109375 to 0.109375
- segments: int32 [8, 512], P('dp'), may hold values from 0 to 3, never falling along the last dimension, each value on 1 to 256 neighbouring positions
- cotangent: bfloat16 [4096, 768], P(('dp', 'tensor')), may hold values from -6 to 6
Outputs:
- block_out: bfloat16 [4096, 768], P(('dp', 'tensor'))
- block_input_gradient: bfloat16 [4096, 768], P(('dp', 'tensor'))
- ln_gain_grad: float32 [2, 768], P(None, ('dp', 'tensor'))
- ln_bias_grad: float32 [2, 768], P(None, ('dp', 'tensor'))
- w_qkv_grad: float32 [3, 768, 768], P(None, 'dp', 'tensor')
- qv_bias_grad: float32 [2, 768], P(None, ('dp', 'tensor'))
- w_out_grad: float32 [768, 768], P('tensor', 'dp')
- res_bias_grad: float32 [2, 768], P(None, ('dp', 'tensor'))
- w_fc_grad: float32 [768, 3072], P('dp', 'tensor')
- fc_bias_grad: float32 [3072], P(('dp', 'tensor'))
- w_proj_grad: float32 [3072, 768], P('tensor', 'dp')
The draws below stay inside these ranges and needn't reach their ends.
Inputs may be any that keep to these rules, and one draw needn't show every extreme that they name: `segments`: in each sequence the document numbers never fall, so every document is a contiguous run of tokens.
All inputs are finite; a program needn't handle non-finite values.
Results may differ from the reference program's by a relative error of at most 0.012.
Values may be sent and summed in bfloat16 or wider, within the bound.
A program may use at most 64 MiB of HBM per device.

```python
import math
import jax
import jax.numpy as jnp
import numpy as np
from jax import lax

D = 768
HEADS = 12
HEAD_DIM = 64
FF = 3072
LEN = 512
SEQ_DEV = 1
SEG_COUNT = 4
SEQS = 8
TOKENS = 4096


def block_levels(key, dims, cuts, smallest, high):
    def one(axis_at, shards_of):
        heights = jax.random.uniform(jax.random.fold_in(jax.random.fold_in(key, 6), axis_at), (shards_of,), jnp.float32, smallest / len(cuts), high / len(cuts))
        return jnp.repeat(jnp.exp(heights), dims[axis_at] // shards_of).reshape((-1,) + (1,) * (len(dims) - axis_at - 1))

    gain = one(*cuts[0])
    for cut in cuts[1:]:
        gain = gain * one(*cut)
    return gain


def profile(number_of, total, bound, slope):
    loads = [(1 << 20) // math.isqrt(rank ** slope) + 1 for rank in range(2, number_of + 1)]
    rest, counts = total - bound - (number_of - 1), [1] * (number_of - 1)
    while rest > 0:
        movable = [i for i in range(number_of - 1) if counts[i] < bound]
        pool, remaining = sum([loads[i] for i in movable]), rest
        for i in movable:
            extra = min(bound - counts[i], max(1, remaining * loads[i] // pool), rest)
            counts[i] = counts[i] + extra
            rest = rest - extra
    return np.array([bound] + counts)


def ragged(stream_key, number_of, total, reach, skew):
    if number_of == 2:
        one = jax.random.randint(stream_key, (), max(1, total - reach), min(reach, total - 1) + 1)
        return jnp.stack([one, total - one])
    lengths = jnp.asarray(profile(number_of, total, reach, skew), jnp.int32)
    pairs = (number_of - 1) // 2
    giver, receiver = lengths[1:1 + 2 * pairs:2], lengths[2:2 + 2 * pairs:2]
    room = jnp.minimum(giver - 1, reach - receiver)
    shifted = jax.random.randint(jax.random.fold_in(stream_key, 1), (pairs,), 0, 1 << 20) % (room + 1)
    lengths = lengths.at[1:1 + 2 * pairs:2].set(giver - shifted).at[2:2 + 2 * pairs:2].set(receiver + shifted)
    return lengths[jax.random.permutation(jax.random.fold_in(stream_key, 2), number_of)]


def scatter_about(key, extent, spread, limit, cuts=(), held_as=jnp.bfloat16):
    drawn = spread * jax.random.normal(key, extent, jnp.float32)
    if cuts:
        drawn = drawn * block_levels(key, extent, cuts, -0.22, 0.18)
    return jnp.clip(drawn, -limit, limit).astype(held_as)


def setup_inputs(seed: int = 0) -> dict:
    splits = jax.random.split(jax.random.key(seed), 13)
    tokens = scatter_about(splits[0], (TOKENS, D), 1.0, 6.0, ((0, 32),))
    norm_gain_pair = jnp.clip(1.0 + 0.1 * jax.random.normal(splits[1], (2, D), jnp.float32), 0.5, 1.5)
    norm_bias_pair = scatter_about(splits[2], (2, D), 0.5, 3.0, ((1, 32),), jnp.float32)
    w_qkv = scatter_about(splits[3], (3, D, D), D ** -0.5, 0.21875, ((1, 8), (2, 4)))
    qv_bias = scatter_about(splits[4], (2, D), 0.5, 3.0, ((1, 32),), jnp.float32)
    w_out = scatter_about(splits[5], (D, D), (D // 16) ** -0.5, 0.875, ((0, 4), (1, 8)))
    res_bias = scatter_about(splits[6], (2, D), 0.5, 3.0, ((1, 32),), jnp.float32)
    w_fc = scatter_about(splits[7], (D, FF), D ** -0.5, 0.21875, ((0, 8), (1, 4)))
    fc_bias = scatter_about(splits[8], (FF,), 0.5, 3.0, ((0, 32),), jnp.float32)
    w_proj = scatter_about(splits[9], (FF, D), FF ** -0.5, 0.109375, ((0, 4), (1, 8)))
    segments = jax.vmap(lambda own: jnp.searchsorted(jnp.cumsum(ragged(own, SEG_COUNT, LEN, LEN // 2, 0)), jnp.arange(LEN), side="right"))(jax.random.split(splits[10], SEQS)).reshape((SEQS, LEN)).astype(jnp.int32)
    cotangent = scatter_about(splits[11], (TOKENS, D), 1.0, 6.0, ((0, 32),))
    return {"tokens": tokens, "norm_gain_pair": norm_gain_pair, "norm_bias_pair": norm_bias_pair, "w_qkv": w_qkv, "qv_bias": qv_bias, "w_out": w_out, "res_bias": res_bias, "w_fc": w_fc, "fc_bias": fc_bias, "w_proj": w_proj, "segments": segments, "cotangent": cotangent}


epsilon = 1e-05
gelu_coeff = 0.044715
gelu_root = 0.7978845608028654

def layer_normalize(rows, norm_gain, norm_shift):
    centered_input = rows - lax.optimization_barrier(jnp.mean(rows, axis=-1, keepdims=True))
    inverse_deviation = lax.rsqrt(lax.optimization_barrier(jnp.mean(centered_input * centered_input, axis=-1, keepdims=True)) + epsilon)
    standardized_input = centered_input * inverse_deviation
    return (standardized_input * norm_gain + norm_shift, standardized_input, inverse_deviation)

def layer_normalize_backward(output_gradient, standardized_input, inverse_deviation, norm_gain):
    scaled_rows = output_gradient * norm_gain
    return inverse_deviation * (scaled_rows - lax.optimization_barrier(jnp.mean(scaled_rows, axis=-1, keepdims=True)) - standardized_input * lax.optimization_barrier(jnp.mean(scaled_rows * standardized_input, axis=-1, keepdims=True)))

def gelu_value(pre):
    return 0.5 * pre * (1.0 + jnp.tanh(gelu_root * (pre + gelu_coeff * pre * pre * pre)))

def gelu_slope(pre):
    tangent = jnp.tanh(gelu_root * (pre + gelu_coeff * pre * pre * pre))
    return 0.5 * (1.0 + tangent) + 0.5 * pre * (1.0 - tangent * tangent) * gelu_root * (1.0 + 3.0 * gelu_coeff * pre * pre)

def allowed_pairs(segment):
    length = segment.shape[0]
    rows = lax.broadcasted_iota(jnp.int32, (length, length), 0)
    cols = lax.broadcasted_iota(jnp.int32, (length, length), 1)
    return (segment[:, None] == segment[None, :]) & (rows >= cols)

def masked_scores(query, key, segment):
    scores = jnp.einsum('qhd,khd->hqk', query.astype(jnp.float32), key.astype(jnp.float32)) * HEAD_DIM ** (-0.5)
    return jnp.where(allowed_pairs(segment)[None], scores, -1e+30)

def attend(query, key, value, segment):
    scores = masked_scores(query, key, segment)
    peak = lax.optimization_barrier(jnp.max(scores, axis=-1, keepdims=True))
    logsum = peak + jnp.log(lax.optimization_barrier(jnp.sum(jnp.exp(scores - peak), axis=-1, keepdims=True)))
    weights = jnp.exp(scores - logsum).astype(jnp.bfloat16)
    context = jnp.einsum('hqk,khd->qhd', weights.astype(jnp.float32), value.astype(jnp.float32))
    return (context.astype(jnp.bfloat16), logsum)

def attend_back(query, key, value, segment, logsum, grad_context):
    probs = jnp.exp(masked_scores(query, key, segment) - logsum)
    probs_half = probs.astype(jnp.bfloat16).astype(jnp.float32)
    grad_ctx = grad_context.astype(jnp.float32)
    grad_value = jnp.einsum('hqk,qhd->khd', probs_half, grad_ctx)
    grad_probs = jnp.einsum('qhd,khd->hqk', grad_ctx, value.astype(jnp.float32))
    inner = lax.optimization_barrier(jnp.sum(probs * grad_probs, axis=-1, keepdims=True))
    grad_scores = (probs * (grad_probs - inner)).astype(jnp.bfloat16).astype(jnp.float32)
    grad_query = jnp.einsum('hqk,khd->qhd', grad_scores, key.astype(jnp.float32)) * HEAD_DIM ** (-0.5)
    grad_key = jnp.einsum('hqk,qhd->khd', grad_scores, query.astype(jnp.float32)) * HEAD_DIM ** (-0.5)
    return (grad_query, grad_key, grad_value)

def contract_rows(left, right):
    return lax.dot_general(left, right, (((0,), (0,)), ((), ())), preferred_element_type=jnp.float32)

def contract_cols(left, right):
    return lax.dot_general(left, right, (((1,), (1,)), ((), ())), preferred_element_type=jnp.float32)

def block_pass(params, pieces):
    norm_gain_pair, norm_bias_pair, w_qkv, qv_bias, w_out, res_bias, w_fc, fc_bias, w_proj = params
    tokens, segments, cotangent = pieces
    count_rows = tokens.shape[0]
    residual_stream = tokens.astype(jnp.float32)
    first_norm_output, first_standardized, first_inverse_deviation = layer_normalize(residual_stream, norm_gain_pair[0], norm_bias_pair[0])
    first_norm_output = first_norm_output.astype(jnp.bfloat16)
    query = (jnp.dot(first_norm_output, w_qkv[0], preferred_element_type=jnp.float32) + qv_bias[0]).astype(jnp.bfloat16)
    keys = jnp.dot(first_norm_output, w_qkv[1], preferred_element_type=jnp.float32).astype(jnp.bfloat16)
    value = (jnp.dot(first_norm_output, w_qkv[2], preferred_element_type=jnp.float32) + qv_bias[1]).astype(jnp.bfloat16)

    def split(array):
        return array.reshape(SEQ_DEV, LEN, HEADS, HEAD_DIM)
    context, logsum = jax.vmap(attend)(split(query), split(keys), split(value), segments)
    context = context.reshape(count_rows, D)
    first_hidden = residual_stream + jnp.dot(context, w_out, preferred_element_type=jnp.float32) + res_bias[0]
    second_norm_output, second_standardized, second_inverse_deviation = layer_normalize(first_hidden, norm_gain_pair[1], norm_bias_pair[1])
    second_norm_output = second_norm_output.astype(jnp.bfloat16)
    pre = jnp.dot(second_norm_output, w_fc, preferred_element_type=jnp.float32) + fc_bias
    act = gelu_value(pre).astype(jnp.bfloat16)
    block_out = (first_hidden + jnp.dot(act, w_proj, preferred_element_type=jnp.float32) + res_bias[1]).astype(jnp.bfloat16)
    residual_gradient = cotangent.astype(jnp.float32)
    proj_grad = contract_rows(act, cotangent)
    res1_grad = lax.optimization_barrier(jnp.sum(residual_gradient, axis=0))
    d_pre = contract_cols(cotangent, w_proj) * gelu_slope(pre)
    fcb_grad = lax.optimization_barrier(jnp.sum(d_pre, axis=0))
    d_pre_half = d_pre.astype(jnp.bfloat16)
    fc_grad = contract_rows(second_norm_output, d_pre_half)
    second_norm_gradient = contract_cols(d_pre_half, w_fc)
    second_gain_gradient = lax.optimization_barrier(jnp.sum(second_norm_gradient * second_standardized, axis=0))
    shift2_grad = lax.optimization_barrier(jnp.sum(second_norm_gradient, axis=0))
    first_hidden_gradient = residual_gradient + layer_normalize_backward(second_norm_gradient, second_standardized, second_inverse_deviation, norm_gain_pair[1])
    res0_grad = lax.optimization_barrier(jnp.sum(first_hidden_gradient, axis=0))
    d_hidden1_half = first_hidden_gradient.astype(jnp.bfloat16)
    out_grad = contract_rows(context, d_hidden1_half)
    d_context = contract_cols(d_hidden1_half, w_out).astype(jnp.bfloat16)
    grad_query, grad_key, grad_value = jax.vmap(attend_back)(split(query), split(keys), split(value), segments, logsum, split(d_context))
    grad_query = grad_query.reshape(count_rows, D)
    grad_key = grad_key.reshape(count_rows, D)
    grad_value = grad_value.reshape(count_rows, D)
    qb_grad = lax.optimization_barrier(jnp.sum(grad_query, axis=0))
    vb_grad = lax.optimization_barrier(jnp.sum(grad_value, axis=0))
    d_qkv = jnp.stack([grad_query, grad_key, grad_value]).astype(jnp.bfloat16)
    qkv_grad = jnp.stack([contract_rows(first_norm_output, d_qkv[index]) for index in range(3)])
    first_norm_gradient = contract_cols(d_qkv[0], w_qkv[0]) + contract_cols(d_qkv[1], w_qkv[1]) + contract_cols(d_qkv[2], w_qkv[2])
    first_gain_gradient = lax.optimization_barrier(jnp.sum(first_norm_gradient * first_standardized, axis=0))
    shift1_grad = lax.optimization_barrier(jnp.sum(first_norm_gradient, axis=0))
    block_input_gradient = (first_hidden_gradient + layer_normalize_backward(first_norm_gradient, first_standardized, first_inverse_deviation, norm_gain_pair[0])).astype(jnp.bfloat16)
    grads = (jnp.stack([first_gain_gradient, second_gain_gradient]), jnp.stack([shift1_grad, shift2_grad]), qkv_grad, jnp.stack([qb_grad, vb_grad]), out_grad, jnp.stack([res0_grad, res1_grad]), fc_grad, fcb_grad, proj_grad)
    return ((block_out, block_input_gradient), grads)

def reference(tokens, norm_gain_pair, norm_bias_pair, w_qkv, qv_bias, w_out, res_bias, w_fc, fc_bias, w_proj, segments, cotangent):
    params = (norm_gain_pair, norm_bias_pair, w_qkv, qv_bias, w_out, res_bias, w_fc, fc_bias, w_proj)
    groups = SEQS // SEQ_DEV
    rows = SEQ_DEV * LEN
    tok_blocks = tokens.reshape(groups, rows, D)
    seg_blocks = segments.reshape(groups, SEQ_DEV, LEN)
    cot_blocks = cotangent.reshape(groups, rows, D)
    start = (jnp.zeros((2, D), jnp.float32), jnp.zeros((2, D), jnp.float32), jnp.zeros((3, D, D), jnp.float32), jnp.zeros((2, D), jnp.float32), jnp.zeros((D, D), jnp.float32), jnp.zeros((2, D), jnp.float32), jnp.zeros((D, FF), jnp.float32), jnp.zeros((FF,), jnp.float32), jnp.zeros((FF, D), jnp.float32))

    def step(carry, pieces):
        outputs, grads = block_pass(params, pieces)
        return (tuple((total + part for total, part in zip(carry, grads))), outputs)
    totals, (outs, in_grads) = lax.scan(step, start, (tok_blocks, seg_blocks, cot_blocks))
    return (outs.reshape(TOKENS, D), in_grads.reshape(TOKENS, D), totals[0], totals[1], totals[2], totals[3], totals[4], totals[5], totals[6], totals[7], totals[8])
```

```python
import functools

import jax
import jax.numpy as jnp
from jax import lax
from jax.experimental import pallas as pl
from jax.experimental.pallas import tpu as pltpu
from jax.sharding import PartitionSpec as P

HEAD_DIM = 64


epsilon = 1e-05
gelu_coeff = 0.044715
gelu_root = 0.7978845608028654


def layer_normalize(rows, norm_gain, norm_shift):
    centered_input = rows - jnp.mean(rows, axis=-1, keepdims=True)
    inverse_deviation = lax.rsqrt(
        jnp.mean(centered_input * centered_input, axis=-1, keepdims=True) + epsilon
    )
    standardized_input = centered_input * inverse_deviation
    return (standardized_input * norm_gain + norm_shift, standardized_input, inverse_deviation)


def layer_normalize_backward(output_gradient, standardized_input, inverse_deviation, norm_gain):
    scaled_rows = output_gradient * norm_gain
    return inverse_deviation * (
        scaled_rows
        - jnp.mean(scaled_rows, axis=-1, keepdims=True)
        - standardized_input * jnp.mean(scaled_rows * standardized_input, axis=-1, keepdims=True)
    )


def gelu_value(pre):
    return 0.5 * pre * (1.0 + jnp.tanh(gelu_root * (pre + gelu_coeff * pre * pre * pre)))


def gelu_slope(pre):
    tangent = jnp.tanh(gelu_root * (pre + gelu_coeff * pre * pre * pre))
    return 0.5 * (1.0 + tangent) + 0.5 * pre * (1.0 - tangent * tangent) * gelu_root * (
        1.0 + 3.0 * gelu_coeff * pre * pre
    )


def allowed_pairs(segment):
    length = segment.shape[0]
    rows = lax.broadcasted_iota(jnp.int32, (length, length), 0)
    cols = lax.broadcasted_iota(jnp.int32, (length, length), 1)
    return (segment[:, None] == segment[None, :]) & (rows >= cols)


def masked_scores(query, key, segment):
    scores = jnp.einsum(
        "qhd,khd->hqk", query, key, preferred_element_type=jnp.float32
    ) * HEAD_DIM ** (-0.5)
    return jnp.where(allowed_pairs(segment)[None], scores, -1e30)


def attend(pieces):
    query, key, value, segment = pieces
    scores = masked_scores(query, key, segment)
    peak = jnp.max(scores, axis=-1, keepdims=True)
    logsum = peak + jnp.log(jnp.sum(jnp.exp(scores - peak), axis=-1, keepdims=True))
    weights = jnp.exp(scores - logsum).astype(jnp.bfloat16)
    context = jnp.einsum("hqk,khd->qhd", weights, value, preferred_element_type=jnp.float32)
    return (context.astype(jnp.bfloat16), logsum)


def attend_back(pieces):
    query, key, value, segment, logsum, grad_context = pieces
    probs = jnp.exp(masked_scores(query, key, segment) - logsum)
    probs_half = probs.astype(jnp.bfloat16)
    grad_value = jnp.einsum(
        "hqk,qhd->khd", probs_half, grad_context, preferred_element_type=jnp.float32
    )
    grad_probs = jnp.einsum("qhd,khd->hqk", grad_context, value, preferred_element_type=jnp.float32)
    inner = jnp.sum(probs * grad_probs, axis=-1, keepdims=True)
    grad_scores = (probs * (grad_probs - inner)).astype(jnp.bfloat16)
    grad_query = jnp.einsum(
        "hqk,khd->qhd", grad_scores, key, preferred_element_type=jnp.float32
    ) * HEAD_DIM ** (-0.5)
    grad_key = jnp.einsum(
        "hqk,qhd->khd", grad_scores, query, preferred_element_type=jnp.float32
    ) * HEAD_DIM ** (-0.5)
    return (grad_query, grad_key, grad_value)


def contract_rows(left, right):
    return lax.dot_general(
        left, right, (((0,), (0,)), ((), ())), preferred_element_type=jnp.float32
    )


def contract_cols(left, right):
    return lax.dot_general(
        left, right, (((1,), (1,)), ((), ())), preferred_element_type=jnp.float32
    )


MESH = pl.DeviceIdType.MESH


def loop(count, body):
    if count <= 8:
        for step in range(count):
            body(step)
    else:

        def wrapped(step, carry):
            body(step)
            return carry

        lax.fori_loop(0, count, wrapped, 0)


def remote(src, dst, send, recv, device):
    return pltpu.make_async_remote_copy(
        src_ref=src, dst_ref=dst, send_sem=send, recv_sem=recv, device_id=device, device_id_type=MESH
    )


class FlatGather:
    def __init__(self, n, me, device, src, out, sems, local_sem):
        self.n, self.me, self.device, self.src, self.out, self.sems = n, me, device, src, out, sems
        self.local = pltpu.make_async_copy(src, out.at[me], local_sem)

    def copy(self, step):
        k = step + 1
        return remote(
            self.src,
            self.out.at[self.me],
            self.sems.at[0, k],
            self.sems.at[1, k],
            self.device(lax.rem(self.me + k, self.n)),
        )

    def start(self):
        loop(self.n - 1, lambda step: self.copy(step).start())
        self.local.start()

    def middle(self):
        pass

    def finish(self):
        loop(self.n - 1, lambda step: self.copy(step).wait())
        self.local.wait()


class PairGather:
    def __init__(self, n, me, device, src, out, sems, local_sem):
        self.n, self.me, self.device, self.src, self.out, self.sems = n, me, device, src, out, sems
        self.chips, self.core = n // 2, lax.rem(me, 2)
        self.chip = me // 2
        self.sibling = self.chip * 2 + 1 - self.core
        self.local = pltpu.make_async_copy(src, out.at[me], local_sem)

    def across(self, step):
        k = step + 1
        peer = lax.rem(self.chip + k, self.chips) * 2 + self.core
        return remote(
            self.src,
            self.out.at[self.me],
            self.sems.at[0, k],
            self.sems.at[1, k],
            self.device(peer),
        )

    def to_sibling(self):
        return remote(
            self.src,
            self.out.at[self.me],
            self.sems.at[0, 0],
            self.sems.at[1, 0],
            self.device(self.sibling),
        )

    def hand(self, step):
        k = step + 1
        slot = lax.rem(self.chip + self.chips - k, self.chips) * 2 + self.core
        return remote(
            self.out.at[slot],
            self.out.at[slot],
            self.sems.at[2, k],
            self.sems.at[3, k],
            self.device(self.sibling),
        )

    def start(self):
        loop(self.chips - 1, lambda step: self.across(step).start())
        self.to_sibling().start()
        self.local.start()

    def middle(self):
        def step_through(step):
            self.across(step).wait_recv()
            self.hand(step).start()

        loop(self.chips - 1, step_through)

    def finish(self):
        loop(self.chips - 1, lambda step: self.across(step).wait_send())
        self.to_sibling().wait()
        loop(self.chips - 1, lambda step: self.hand(step).wait())
        self.local.wait()


class FlatSum:
    def __init__(self, n, me, device, src, out, sems, slots):
        self.n, self.me, self.device, self.src, self.out, self.sems = n, me, device, src, out, sems
        self.slots = slots

    def copy(self, step):
        k = step + 1
        peer = lax.rem(self.me + k, self.n)
        return remote(
            self.src.at[peer],
            self.slots.at[k],
            self.sems.at[0, k],
            self.sems.at[1, k],
            self.device(peer),
        )

    def start(self):
        loop(self.n - 1, lambda step: self.copy(step).start())

    def middle(self):
        pass

    def finish(self):
        self.out[...] = self.src[self.me].astype(jnp.float32)

        def add(step):
            self.copy(step).wait()
            self.out[...] += self.slots[step + 1].astype(jnp.float32)

        loop(self.n - 1, add)


class PairSum:
    def __init__(self, n, me, device, src, out, sems, slots, sums):
        self.n, self.me, self.device, self.src, self.out, self.sems = n, me, device, src, out, sems
        self.slots, self.sums = slots, sums
        self.chips, self.core = n // 2, lax.rem(me, 2)
        self.chip = me // 2
        self.sibling = self.chip * 2 + 1 - self.core

    def trade(self, step):
        target = lax.rem(self.chip + step + 1, self.chips)
        return remote(
            self.src.at[target * 2 + 1 - self.core],
            self.slots.at[step],
            self.sems.at[0, step],
            self.sems.at[1, step],
            self.device(self.sibling),
        )

    def across(self, step):
        target = lax.rem(self.chip + step + 1, self.chips)
        return remote(
            self.sums.at[step],
            self.slots.at[self.chips + step],
            self.sems.at[2, step],
            self.sems.at[3, step],
            self.device(target * 2 + self.core),
        )

    def start(self):
        loop(self.chips, lambda step: self.trade(step).start())

    def middle(self):
        def pair(step):
            target = lax.rem(self.chip + step + 1, self.chips)
            self.trade(step).wait_recv()
            return self.src[target * 2 + self.core].astype(jnp.float32) + self.slots[step].astype(
                jnp.float32
            )

        def forward(step):
            self.sums[step] = pair(step).astype(self.sums.dtype)
            self.across(step).start()

        loop(self.chips - 1, forward)
        self.out[...] = pair(self.chips - 1)

    def finish(self):
        loop(self.chips, lambda step: self.trade(step).wait_send())

        def add(step):
            self.across(step).wait()
            self.out[...] += self.slots[self.chips + step].astype(jnp.float32)

        loop(self.chips - 1, add)


def exchange(dp, tensor, identity, ops):
    sizes = {"dp": dp, "tensor": tensor, "all": dp * tensor}
    arrays = [array for _, _, array in ops]
    outs, scratch, counts = [], [], []
    for form, axis, array in ops:
        n = sizes[axis]
        mine = [pltpu.SemaphoreType.DMA((4, n))]
        if form in (FlatGather, PairGather):
            outs.append(jax.ShapeDtypeStruct((n,) + array.shape, array.dtype))
            mine.append(pltpu.SemaphoreType.DMA)
        else:
            outs.append(jax.ShapeDtypeStruct(array.shape[1:], jnp.float32))
            mine.append(pltpu.VMEM(array.shape, array.dtype))
            if form is PairSum:
                mine.append(pltpu.VMEM((n // 2,) + array.shape[1:], array.dtype))
        scratch += mine
        counts.append(len(mine))
    axes = {axis for _, axis, _ in ops}

    def kernel(*refs):
        sources = refs[: len(ops)]
        results = refs[len(ops) : 2 * len(ops)]
        rest = list(refs[2 * len(ops) :])
        d, t = lax.axis_index("dp"), lax.axis_index("tensor")
        ranks = {"dp": d, "tensor": t, "all": d * tensor + t}
        devices = {
            "dp": lambda i: {"dp": i, "tensor": t},
            "tensor": lambda i: {"dp": d, "tensor": i},
            "all": lambda i: {"dp": i // tensor, "tensor": lax.rem(i, tensor)},
        }
        barrier = pltpu.get_barrier_semaphore()
        for axis in ["all"] if "all" in axes else sorted(axes):
            n = sizes[axis]

            def greet(step, n=n, axis=axis):
                pl.semaphore_signal(
                    barrier,
                    inc=1,
                    device_id=devices[axis](lax.rem(ranks[axis] + step + 1, n)),
                    device_id_type=MESH,
                )

            loop(n - 1, greet)
        pl.semaphore_wait(
            barrier,
            sizes["all"] - 1 if "all" in axes else sum(sizes[axis] - 1 for axis in axes),
        )
        work = []
        for (form, axis, _), src, out, count in zip(ops, sources, results, counts):
            work.append(form(sizes[axis], ranks[axis], devices[axis], src, out, *rest[:count]))
            del rest[:count]
        for op in work:
            op.start()
        for op in work:
            op.middle()
        for op in work:
            op.finish()

    return pl.pallas_call(
        kernel,
        out_shape=tuple(outs),
        in_specs=[pl.BlockSpec(memory_space=pltpu.VMEM)] * len(ops),
        out_specs=tuple([pl.BlockSpec(memory_space=pltpu.VMEM)] * len(ops)),
        scratch_shapes=scratch,
        compiler_params=pltpu.CompilerParams(
            collective_id=identity, has_side_effects=True, vmem_limit_bytes=40 * 2**20
        ),
        name="exchange_%d" % identity,
    )(*arrays)


def pad_to(array, axis, size):
    widths = [(0, 0)] * array.ndim
    widths[axis] = (0, size - array.shape[axis])
    return jnp.pad(array, widths) if size > array.shape[axis] else array


def standardize(rows):
    centered = rows - jnp.mean(rows, axis=-1, keepdims=True)
    inverse = lax.rsqrt(jnp.mean(centered * centered, axis=-1, keepdims=True) + epsilon)
    return centered * inverse, inverse


def shards(
    dp,
    tensor,
    tokens,
    norm_gain_pair,
    norm_bias_pair,
    w_qkv,
    qv_bias,
    w_out,
    res_bias,
    w_fc,
    fc_bias,
    w_proj,
    segments,
    cotangent,
):
    place = lax.axis_index("tensor")
    devices = dp * tensor
    width = tokens.shape[1]
    rows_own = w_qkv.shape[1]
    rows_pad = -(-rows_own // 16) * 16
    local_width = w_qkv.shape[2]
    local_hidden = w_fc.shape[1]
    seqs, length = segments.shape
    heads_local = local_width // HEAD_DIM
    head_start = place * local_width
    hidden_start = place * local_hidden
    small = norm_gain_pair.shape[1]
    fc_rows = fc_bias.shape[0] // small
    half = jnp.bfloat16

    attention_weights = jnp.concatenate([w_qkv[0], w_qkv[1], w_qkv[2], w_out.T], axis=1)
    tiny = jnp.concatenate(
        [norm_gain_pair, norm_bias_pair, qv_bias, res_bias, fc_bias.reshape(fc_rows, small)], axis=0
    )
    tiny = pad_to(pad_to(tiny, 1, 128), 0, 16)
    tokens_all, cot_all, w_attn, w_fc_all, w_proj_all, tiny_all = exchange(
        dp,
        tensor,
        1,
        [
            (FlatGather, "tensor", tokens),
            (FlatGather, "tensor", cotangent),
            (PairGather, "dp", pad_to(attention_weights, 0, rows_pad)),
            (PairGather, "dp", pad_to(w_fc, 0, rows_pad)),
            (PairGather, "dp", pad_to(w_proj.T, 0, rows_pad)),
            (FlatGather, "all", tiny),
        ],
    )
    rows_all = tokens.shape[0] * tensor
    tokens_all = tokens_all.reshape(rows_all, width)
    cot_all = cot_all.reshape(rows_all, width)
    w_attn = w_attn[:, :rows_own].reshape(width, 4 * local_width)
    w_fc_all = w_fc_all[:, :rows_own].reshape(width, local_hidden)
    w_proj_all = w_proj_all[:, :rows_own].reshape(width, local_hidden)
    w_in, w_out_t = w_attn[:, : 3 * local_width], w_attn[:, 3 * local_width :]
    vectors = tiny_all[:, :8, :small].transpose(1, 0, 2).reshape(8, width)
    norm_gains, norm_shifts, qv_whole, res_whole = (
        vectors[0:2],
        vectors[2:4],
        vectors[4:6],
        vectors[6:8],
    )
    qv_local = lax.dynamic_slice_in_dim(qv_whole, head_start, local_width, 1)
    fc_local = lax.dynamic_slice_in_dim(tiny_all, place * dp, dp, 0)[
        :, 8 : 8 + fc_rows, :small
    ].reshape(local_hidden)

    xhat1_all, _ = standardize(tokens_all.astype(jnp.float32))
    ln1_all = (xhat1_all * norm_gains[0] + norm_shifts[0]).astype(half)
    residual_stream = tokens.astype(jnp.float32)
    first_standardized, first_inverse_deviation = standardize(residual_stream)
    qkv = jnp.dot(ln1_all, w_in, preferred_element_type=jnp.float32)
    bias3 = jnp.concatenate([qv_local[0], jnp.zeros_like(qv_local[0]), qv_local[1]])
    qkv = (qkv + bias3).astype(half)

    def split(array):
        return array.reshape(seqs, length, heads_local, HEAD_DIM)

    query, keys, value = (
        split(qkv[:, i * local_width : (i + 1) * local_width]) for i in range(3)
    )
    context, logsum = lax.map(attend, (query, keys, value, segments))
    context = context.reshape(rows_all, local_width)
    attn_part = contract_cols(context, w_out_t).astype(half)
    (attn_sum,) = exchange(
        dp, tensor, 2, [(FlatSum, "tensor", attn_part.reshape(tensor, -1, width))]
    )
    first_hidden = residual_stream + attn_sum + res_whole[0]
    second_standardized, second_inverse_deviation = standardize(first_hidden)
    ln2 = (second_standardized * norm_gains[1] + norm_shifts[1]).astype(half)
    (ln2_all,) = exchange(dp, tensor, 3, [(FlatGather, "tensor", ln2)])
    ln2_all = ln2_all.reshape(rows_all, width)
    pre = jnp.dot(ln2_all, w_fc_all, preferred_element_type=jnp.float32) + fc_local
    act = gelu_value(pre).astype(half)
    mlp_part = contract_cols(act, w_proj_all).astype(half)
    d_pre = jnp.dot(cot_all, w_proj_all, preferred_element_type=jnp.float32) * gelu_slope(pre)
    fcb_grad = jnp.sum(d_pre, axis=0)
    d_pre_half = d_pre.astype(half)
    d_ln2_part = contract_cols(d_pre_half, w_fc_all).astype(half)
    proj_grad = contract_rows(cot_all, act).astype(half)
    fc_grad = contract_rows(ln2_all, d_pre_half).astype(half)

    def blocks(array):
        return pad_to(array.reshape(dp, rows_own, array.shape[1]), 1, rows_pad)

    d_ln2, mlp_sum, proj_part, fc_part = exchange(
        dp,
        tensor,
        4,
        [
            (FlatSum, "tensor", d_ln2_part.reshape(tensor, -1, width)),
            (FlatSum, "tensor", mlp_part.reshape(tensor, -1, width)),
            (PairSum, "dp", blocks(proj_grad)),
            (PairSum, "dp", blocks(fc_grad)),
        ],
    )
    block_out = (first_hidden + mlp_sum + res_whole[1]).astype(half)
    residual_gradient = cotangent.astype(jnp.float32)
    res1_grad = jnp.sum(residual_gradient, axis=0)
    second_gain_gradient = jnp.sum(d_ln2 * second_standardized, axis=0)
    shift2_grad = jnp.sum(d_ln2, axis=0)
    first_hidden_gradient = residual_gradient + layer_normalize_backward(
        d_ln2, second_standardized, second_inverse_deviation, norm_gains[1]
    )
    res0_grad = jnp.sum(first_hidden_gradient, axis=0)
    (d_hidden_all,) = exchange(
        dp, tensor, 5, [(FlatGather, "tensor", first_hidden_gradient.astype(half))]
    )
    d_hidden_all = d_hidden_all.reshape(rows_all, width)
    out_grad = contract_rows(d_hidden_all, context)
    d_context = jnp.dot(d_hidden_all, w_out_t, preferred_element_type=jnp.float32).astype(half)
    grads = lax.map(attend_back, (query, keys, value, segments, logsum, split(d_context)))
    grad_query, grad_key, grad_value = (grad.reshape(rows_all, local_width) for grad in grads)
    qb_grad = jnp.sum(grad_query, axis=0)
    vb_grad = jnp.sum(grad_value, axis=0)
    d_qkv = jnp.concatenate([grad_query, grad_key, grad_value], axis=1).astype(half)
    qkv_grad = contract_rows(ln1_all, d_qkv)
    attn_grad = jnp.concatenate([qkv_grad, out_grad], axis=1).astype(half)
    d_ln1_part = contract_cols(d_qkv, w_in)
    first_gain_gradient = jnp.sum(d_ln1_part * xhat1_all, axis=0)
    shift1_grad = jnp.sum(d_ln1_part, axis=0)

    qv_spread = lax.dynamic_update_slice(
        jnp.zeros((2, width), jnp.float32), jnp.stack([qb_grad, vb_grad]), (0, head_start)
    )
    fc_spread = lax.dynamic_update_slice(
        jnp.zeros((devices, fc_rows, small), jnp.float32),
        fcb_grad.reshape(dp, fc_rows, small),
        (place * dp, 0, 0),
    )
    vector_grads = jnp.stack(
        [
            first_gain_gradient,
            second_gain_gradient,
            shift1_grad,
            shift2_grad,
            qv_spread[0],
            qv_spread[1],
            res0_grad,
            res1_grad,
        ]
    )
    tiny_grads = jnp.concatenate(
        [vector_grads.reshape(8, devices, small).transpose(1, 0, 2), fc_spread], axis=1
    )
    tiny_grads = pad_to(pad_to(tiny_grads, 2, 128), 1, 16)
    d_ln1, attn_grad_part, tiny_sum = exchange(
        dp,
        tensor,
        6,
        [
            (FlatSum, "tensor", d_ln1_part.astype(half).reshape(tensor, -1, width)),
            (PairSum, "dp", blocks(attn_grad)),
            (FlatSum, "all", tiny_grads),
        ],
    )
    block_input_gradient = (
        first_hidden_gradient
        + layer_normalize_backward(
            d_ln1, first_standardized, first_inverse_deviation, norm_gains[0]
        )
    ).astype(half)
    attn_grad_part = attn_grad_part[:rows_own]
    qkv_part = jnp.stack(
        [attn_grad_part[:, i * local_width : (i + 1) * local_width] for i in range(3)]
    )
    return (
        block_out,
        block_input_gradient,
        tiny_sum[0:2, :small],
        tiny_sum[2:4, :small],
        qkv_part,
        tiny_sum[4:6, :small],
        attn_grad_part[:, 3 * local_width :].T,
        tiny_sum[6:8, :small],
        fc_part[:rows_own],
        tiny_sum[8 : 8 + fc_rows, :small].reshape(fc_bias.shape[0]),
        proj_part[:rows_own].T,
    )


def solution(mesh):
    return jax.shard_map(
        functools.partial(shards, mesh.shape["dp"], mesh.shape["tensor"]),
        mesh=mesh,
        in_specs=(
            P(("dp", "tensor"), None),
            P(None, ("dp", "tensor")),
            P(None, ("dp", "tensor")),
            P(None, "dp", "tensor"),
            P(None, ("dp", "tensor")),
            P("tensor", "dp"),
            P(None, ("dp", "tensor")),
            P("dp", "tensor"),
            P(("dp", "tensor")),
            P("tensor", "dp"),
            P("dp", None),
            P(("dp", "tensor"), None),
        ),
        out_specs=(
            P(("dp", "tensor"), None),
            P(("dp", "tensor"), None),
            P(None, ("dp", "tensor")),
            P(None, ("dp", "tensor")),
            P(None, "dp", "tensor"),
            P(None, ("dp", "tensor")),
            P("tensor", "dp"),
            P(None, ("dp", "tensor")),
            P("dp", "tensor"),
            P(("dp", "tensor")),
            P("tensor", "dp"),
        ),
        check_vma=False,
    )
```

```python
import functools

import jax
import jax.numpy as jnp
from jax import lax
from jax.experimental import pallas as pl
from jax.experimental.pallas import tpu as pltpu
from jax.sharding import PartitionSpec as P

HEAD_DIM = 64


epsilon = 1e-05
gelu_coeff = 0.044715
gelu_root = 0.7978845608028654


def layer_normalize(rows, norm_gain, norm_shift):
    centered_input = rows - jnp.mean(rows, axis=-1, keepdims=True)
    inverse_deviation = lax.rsqrt(
        jnp.mean(centered_input * centered_input, axis=-1, keepdims=True) + epsilon
    )
    standardized_input = centered_input * inverse_deviation
    return (standardized_input * norm_gain + norm_shift, standardized_input, inverse_deviation)


def layer_normalize_backward(output_gradient, standardized_input, inverse_deviation, norm_gain):
    scaled_rows = output_gradient * norm_gain
    return inverse_deviation * (
        scaled_rows
        - jnp.mean(scaled_rows, axis=-1, keepdims=True)
        - standardized_input * jnp.mean(scaled_rows * standardized_input, axis=-1, keepdims=True)
    )


def gelu_value(pre):
    return 0.5 * pre * (1.0 + jnp.tanh(gelu_root * (pre + gelu_coeff * pre * pre * pre)))


def gelu_slope(pre):
    tangent = jnp.tanh(gelu_root * (pre + gelu_coeff * pre * pre * pre))
    return 0.5 * (1.0 + tangent) + 0.5 * pre * (1.0 - tangent * tangent) * gelu_root * (
        1.0 + 3.0 * gelu_coeff * pre * pre
    )


def allowed_pairs(segment):
    length = segment.shape[0]
    rows = lax.broadcasted_iota(jnp.int32, (length, length), 0)
    cols = lax.broadcasted_iota(jnp.int32, (length, length), 1)
    return (segment[:, None] == segment[None, :]) & (rows >= cols)


def masked_scores(query, key, segment):
    scores = jnp.einsum(
        "qhd,khd->hqk", query, key, preferred_element_type=jnp.float32
    ) * HEAD_DIM ** (-0.5)
    return jnp.where(allowed_pairs(segment)[None], scores, -1e30)


def attend(pieces):
    query, key, value, segment = pieces
    scores = masked_scores(query, key, segment)
    peak = jnp.max(scores, axis=-1, keepdims=True)
    logsum = peak + jnp.log(jnp.sum(jnp.exp(scores - peak), axis=-1, keepdims=True))
    weights = jnp.exp(scores - logsum).astype(jnp.bfloat16)
    context = jnp.einsum("hqk,khd->qhd", weights, value, preferred_element_type=jnp.float32)
    return (context.astype(jnp.bfloat16), logsum)


def attend_back(pieces):
    query, key, value, segment, logsum, grad_context = pieces
    probs = jnp.exp(masked_scores(query, key, segment) - logsum)
    probs_half = probs.astype(jnp.bfloat16)
    grad_value = jnp.einsum(
        "hqk,qhd->khd", probs_half, grad_context, preferred_element_type=jnp.float32
    )
    grad_probs = jnp.einsum("qhd,khd->hqk", grad_context, value, preferred_element_type=jnp.float32)
    inner = jnp.sum(probs * grad_probs, axis=-1, keepdims=True)
    grad_scores = (probs * (grad_probs - inner)).astype(jnp.bfloat16)
    grad_query = jnp.einsum(
        "hqk,khd->qhd", grad_scores, key, preferred_element_type=jnp.float32
    ) * HEAD_DIM ** (-0.5)
    grad_key = jnp.einsum(
        "hqk,qhd->khd", grad_scores, query, preferred_element_type=jnp.float32
    ) * HEAD_DIM ** (-0.5)
    return (grad_query, grad_key, grad_value)


def contract_rows(left, right):
    return lax.dot_general(
        left, right, (((0,), (0,)), ((), ())), preferred_element_type=jnp.float32
    )


def contract_cols(left, right):
    return lax.dot_general(
        left, right, (((1,), (1,)), ((), ())), preferred_element_type=jnp.float32
    )


MESH = pl.DeviceIdType.MESH


def loop(count, body):
    if count <= 8:
        for step in range(count):
            body(step)
    else:

        def wrapped(step, carry):
            body(step)
            return carry

        lax.fori_loop(0, count, wrapped, 0)


def remote(src, dst, send, recv, device):
    return pltpu.make_async_remote_copy(
        src_ref=src, dst_ref=dst, send_sem=send, recv_sem=recv, device_id=device, device_id_type=MESH
    )


class GridGather:
    def __init__(self, dp, tensor, d, t, src, out, sems, local_sem):
        self.dp, self.tensor, self.d, self.t = dp, tensor, d, t
        self.src, self.out, self.sems = src, out, sems
        self.local = pltpu.make_async_copy(src, out.at[d, t], local_sem)

    def first(self, step):
        k = step + 1
        return remote(
            self.src,
            self.out.at[self.d, self.t],
            self.sems.at[0, k],
            self.sems.at[1, k],
            {"dp": self.d, "tensor": lax.rem(self.t + k, self.tensor)},
        )

    def second(self, step):
        k = step + 1
        return remote(
            self.out.at[self.d],
            self.out.at[self.d],
            self.sems.at[2, k],
            self.sems.at[3, k],
            {"dp": lax.rem(self.d + k, self.dp), "tensor": self.t},
        )

    def start(self):
        self.local.start()
        loop(self.tensor - 1, lambda step: self.first(step).start())

    def middle(self):
        self.local.wait()
        loop(self.tensor - 1, lambda step: self.first(step).wait())
        loop(self.dp - 1, lambda step: self.second(step).start())

    def finish(self):
        loop(self.dp - 1, lambda step: self.second(step).wait())


class GridSum:
    def __init__(self, dp, tensor, d, t, src, out, sems, slots, sums):
        self.dp, self.tensor, self.d, self.t = dp, tensor, d, t
        self.src, self.out, self.sems = src, out, sems
        self.slots, self.sums = slots, sums

    def first(self, step):
        k = step + 1
        peer = lax.rem(self.d + k, self.dp)
        return remote(
            self.src.at[peer],
            self.slots.at[k],
            self.sems.at[0, k],
            self.sems.at[1, k],
            {"dp": peer, "tensor": self.t},
        )

    def second(self, step):
        k = step + 1
        peer = lax.rem(self.t + k, self.tensor)
        return remote(
            self.sums.at[0, peer],
            self.sums.at[1, k],
            self.sems.at[2, k],
            self.sems.at[3, k],
            {"dp": self.d, "tensor": peer},
        )

    def start(self):
        loop(self.dp - 1, lambda step: self.first(step).start())

    def middle(self):
        self.sums[0] = self.src[self.d]

        def add(step):
            self.first(step).wait()
            self.sums[0] += self.slots[step + 1]

        loop(self.dp - 1, add)
        loop(self.tensor - 1, lambda step: self.second(step).start())

    def finish(self):
        self.out[...] = self.sums[0, self.t]

        def add(step):
            self.second(step).wait()
            self.out[...] += self.sums[1, step + 1]

        loop(self.tensor - 1, add)


class LineGather:
    def __init__(self, n, me, device, src, out, sems, local_sem):
        self.n, self.me, self.device, self.src, self.out, self.sems = n, me, device, src, out, sems
        self.local = pltpu.make_async_copy(src, out.at[me], local_sem)

    def move(self, side, block, src=None):
        peer = lax.rem(self.me + (1 if side == 0 else self.n - 1), self.n)
        return remote(
            self.out.at[block] if src is None else src,
            self.out.at[block],
            self.sems.at[2 * side, block],
            self.sems.at[2 * side + 1, block],
            self.device(peer),
        )

    def start(self):
        @pl.when(self.me < self.n - 1)
        def _():
            self.move(0, self.me, self.src).start()

        @pl.when(self.me > 0)
        def _():
            self.move(1, self.me, self.src).start()

        self.local.start()

    def middle(self):
        for step in range(1, self.n):

            @pl.when(self.me >= step)
            def _():
                block = self.me - step
                self.move(0, block).wait_recv()

                @pl.when(self.me < self.n - 1)
                def _():
                    self.move(0, block).start()

            @pl.when(self.me + step < self.n)
            def _():
                block = self.me + step
                self.move(1, block).wait_recv()

                @pl.when(self.me > 0)
                def _():
                    self.move(1, block).start()

    def finish(self):
        for step in range(self.n):

            @pl.when((self.me >= step) & (self.me < self.n - 1))
            def _():
                self.move(0, self.me - step).wait_send()

            @pl.when((self.me + step < self.n) & (self.me > 0))
            def _():
                self.move(1, self.me + step).wait_send()

        self.local.wait()


class LineSum:
    def __init__(self, n, me, device, src, out, sems, slots):
        self.n, self.me, self.device, self.src, self.out, self.sems = n, me, device, src, out, sems
        self.slots = slots

    def move(self, side, block, first=False):
        peer = lax.rem(self.me + (1 if side == 0 else self.n - 1), self.n)
        return remote(
            self.src.at[block] if first else self.slots.at[side, block],
            self.slots.at[side, block],
            self.sems.at[2 * side, block],
            self.sems.at[2 * side + 1, block],
            self.device(peer),
        )

    def start(self):
        @pl.when(self.me == 0)
        def _():
            for step in range(self.n - 1):
                self.move(0, self.n - 1 - step, True).start()

        @pl.when(self.me == self.n - 1)
        def _():
            for step in range(self.n - 1):
                self.move(1, step, True).start()

    def forward(self, side, block):
        self.move(side, block).wait_recv()
        self.slots[side, block] = (
            self.slots[side, block].astype(jnp.float32) + self.src[block].astype(jnp.float32)
        ).astype(self.slots.dtype)
        self.move(side, block).start()

    def middle(self):
        for step in range(self.n - 1):

            @pl.when((self.me > 0) & (self.me < self.n - 1 - step))
            def _():
                self.forward(0, self.n - 1 - step)

            @pl.when((self.me < self.n - 1) & (self.me > step))
            def _():
                self.forward(1, step)

    def finish(self):
        self.out[...] = self.src[self.me].astype(jnp.float32)

        @pl.when(self.me > 0)
        def _():
            self.move(0, self.me).wait_recv()
            self.out[...] += self.slots[0, self.me].astype(jnp.float32)

        @pl.when(self.me < self.n - 1)
        def _():
            self.move(1, self.me).wait_recv()
            self.out[...] += self.slots[1, self.me].astype(jnp.float32)

        for block in range(self.n):

            @pl.when(self.me < block)
            def _():
                self.move(0, block).wait_send()

            @pl.when(self.me > block)
            def _():
                self.move(1, block).wait_send()


class PairGather:
    def __init__(self, n, me, device, src, out, sems, local_sem):
        self.n, self.me, self.device, self.src, self.out, self.sems = n, me, device, src, out, sems
        self.chips, self.core = n // 2, lax.rem(me, 2)
        self.chip = me // 2
        self.sibling = self.chip * 2 + 1 - self.core
        self.local = pltpu.make_async_copy(src, out.at[me], local_sem)

    def across(self, step):
        k = step + 1
        peer = lax.rem(self.chip + k, self.chips) * 2 + self.core
        return remote(
            self.src,
            self.out.at[self.me],
            self.sems.at[0, k],
            self.sems.at[1, k],
            self.device(peer),
        )

    def to_sibling(self):
        return remote(
            self.src,
            self.out.at[self.me],
            self.sems.at[0, 0],
            self.sems.at[1, 0],
            self.device(self.sibling),
        )

    def hand(self, step):
        k = step + 1
        slot = lax.rem(self.chip + self.chips - k, self.chips) * 2 + self.core
        return remote(
            self.out.at[slot],
            self.out.at[slot],
            self.sems.at[2, k],
            self.sems.at[3, k],
            self.device(self.sibling),
        )

    def start(self):
        loop(self.chips - 1, lambda step: self.across(step).start())
        self.to_sibling().start()
        self.local.start()

    def middle(self):
        def step_through(step):
            self.across(step).wait_recv()
            self.hand(step).start()

        loop(self.chips - 1, step_through)

    def finish(self):
        loop(self.chips - 1, lambda step: self.across(step).wait_send())
        self.to_sibling().wait()
        loop(self.chips - 1, lambda step: self.hand(step).wait())
        self.local.wait()


class PairSum:
    def __init__(self, n, me, device, src, out, sems, slots, sums):
        self.n, self.me, self.device, self.src, self.out, self.sems = n, me, device, src, out, sems
        self.slots, self.sums = slots, sums
        self.chips, self.core = n // 2, lax.rem(me, 2)
        self.chip = me // 2
        self.sibling = self.chip * 2 + 1 - self.core

    def trade(self, step):
        target = lax.rem(self.chip + step + 1, self.chips)
        return remote(
            self.src.at[target * 2 + 1 - self.core],
            self.slots.at[step],
            self.sems.at[0, step],
            self.sems.at[1, step],
            self.device(self.sibling),
        )

    def across(self, step):
        target = lax.rem(self.chip + step + 1, self.chips)
        return remote(
            self.sums.at[step],
            self.slots.at[self.chips + step],
            self.sems.at[2, step],
            self.sems.at[3, step],
            self.device(target * 2 + self.core),
        )

    def start(self):
        loop(self.chips, lambda step: self.trade(step).start())

    def middle(self):
        def pair(step):
            target = lax.rem(self.chip + step + 1, self.chips)
            self.trade(step).wait_recv()
            return self.src[target * 2 + self.core].astype(jnp.float32) + self.slots[step].astype(
                jnp.float32
            )

        def forward(step):
            self.sums[step] = pair(step).astype(self.sums.dtype)
            self.across(step).start()

        loop(self.chips - 1, forward)
        self.out[...] = pair(self.chips - 1)

    def finish(self):
        loop(self.chips, lambda step: self.trade(step).wait_send())

        def add(step):
            self.across(step).wait()
            self.out[...] += self.slots[self.chips + step].astype(jnp.float32)

        loop(self.chips - 1, add)


def exchange(dp, tensor, identity, ops):
    sizes = {"dp": dp, "tensor": tensor, "all": dp * tensor}
    arrays = [array for _, _, array in ops]
    outs, scratch, counts = [], [], []
    for form, axis, array in ops:
        n = sizes[axis]
        mine = [pltpu.SemaphoreType.DMA((4, max(dp, tensor) if axis == "all" else n))]
        if form is GridGather:
            outs.append(jax.ShapeDtypeStruct((dp, tensor) + array.shape, array.dtype))
            mine.append(pltpu.SemaphoreType.DMA)
        elif form in (LineGather, PairGather):
            outs.append(jax.ShapeDtypeStruct((n,) + array.shape, array.dtype))
            mine.append(pltpu.SemaphoreType.DMA)
        elif form is GridSum:
            outs.append(jax.ShapeDtypeStruct(array.shape[2:], jnp.float32))
            mine.append(pltpu.VMEM(array.shape, array.dtype))
            mine.append(pltpu.VMEM((2,) + array.shape[1:], array.dtype))
        else:
            outs.append(jax.ShapeDtypeStruct(array.shape[1:], jnp.float32))
            if form is LineSum:
                mine.append(pltpu.VMEM((2,) + array.shape, array.dtype))
            else:
                mine.append(pltpu.VMEM(array.shape, array.dtype))
                mine.append(pltpu.VMEM((n // 2,) + array.shape[1:], array.dtype))
        scratch += mine
        counts.append(len(mine))
    axes = {axis for _, axis, _ in ops}
    if "all" in axes:
        axes = {"dp", "tensor"}

    def kernel(*refs):
        sources = refs[: len(ops)]
        results = refs[len(ops) : 2 * len(ops)]
        rest = list(refs[2 * len(ops) :])
        d, t = lax.axis_index("dp"), lax.axis_index("tensor")
        ranks = {"dp": d, "tensor": t}
        devices = {
            "dp": lambda i: {"dp": i, "tensor": t},
            "tensor": lambda i: {"dp": d, "tensor": i},
        }
        barrier = pltpu.get_barrier_semaphore()
        for axis in sorted(axes):
            n = sizes[axis]

            def greet(step, n=n, axis=axis):
                pl.semaphore_signal(
                    barrier,
                    inc=1,
                    device_id=devices[axis](lax.rem(ranks[axis] + step + 1, n)),
                    device_id_type=MESH,
                )

            loop(n - 1, greet)
        pl.semaphore_wait(barrier, sum(sizes[axis] - 1 for axis in axes))
        work = []
        for (form, axis, _), src, out, count in zip(ops, sources, results, counts):
            if axis == "all":
                work.append(form(dp, tensor, d, t, src, out, *rest[:count]))
            else:
                work.append(form(sizes[axis], ranks[axis], devices[axis], src, out, *rest[:count]))
            del rest[:count]
        for op in work:
            op.start()
        order = [GridGather, GridSum, PairSum, LineSum, LineGather, PairGather]
        for op in sorted(work, key=lambda op: order.index(type(op))):
            op.middle()
        for op in work:
            op.finish()

    return pl.pallas_call(
        kernel,
        out_shape=tuple(outs),
        in_specs=[pl.BlockSpec(memory_space=pltpu.VMEM)] * len(ops),
        out_specs=tuple([pl.BlockSpec(memory_space=pltpu.VMEM)] * len(ops)),
        scratch_shapes=scratch,
        compiler_params=pltpu.CompilerParams(
            collective_id=identity, has_side_effects=True, vmem_limit_bytes=40 * 2**20
        ),
        name="exchange_%d" % identity,
    )(*arrays)


def pad_to(array, axis, size):
    widths = [(0, 0)] * array.ndim
    widths[axis] = (0, size - array.shape[axis])
    return jnp.pad(array, widths) if size > array.shape[axis] else array


def standardize(rows):
    centered = rows - jnp.mean(rows, axis=-1, keepdims=True)
    inverse = lax.rsqrt(jnp.mean(centered * centered, axis=-1, keepdims=True) + epsilon)
    return centered * inverse, inverse


def shards(
    dp,
    tensor,
    tokens,
    norm_gain_pair,
    norm_bias_pair,
    w_qkv,
    qv_bias,
    w_out,
    res_bias,
    w_fc,
    fc_bias,
    w_proj,
    segments,
    cotangent,
):
    place = lax.axis_index("tensor")
    devices = dp * tensor
    width = tokens.shape[1]
    rows_own = w_qkv.shape[1]
    rows_pad = -(-rows_own // 16) * 16
    local_width = w_qkv.shape[2]
    local_hidden = w_fc.shape[1]
    seqs, length = segments.shape
    heads_local = local_width // HEAD_DIM
    head_start = place * local_width
    hidden_start = place * local_hidden
    small = norm_gain_pair.shape[1]
    fc_rows = fc_bias.shape[0] // small
    half = jnp.bfloat16

    attention_weights = jnp.concatenate([w_qkv[0], w_qkv[1], w_qkv[2], w_out.T], axis=1)
    tiny = jnp.concatenate(
        [norm_gain_pair, norm_bias_pair, qv_bias, res_bias, fc_bias.reshape(fc_rows, small)], axis=0
    )
    tiny = pad_to(pad_to(tiny, 1, 128), 0, 16)
    tiny_all, tokens_all, cot_all, w_attn, w_fc_all, w_proj_all = exchange(
        dp,
        tensor,
        1,
        [
            (GridGather, "all", tiny),
            (LineGather, "tensor", tokens),
            (LineGather, "tensor", cotangent),
            (PairGather, "dp", pad_to(attention_weights, 0, rows_pad)),
            (PairGather, "dp", pad_to(w_fc, 0, rows_pad)),
            (PairGather, "dp", pad_to(w_proj.T, 0, rows_pad)),
        ],
    )
    rows_all = tokens.shape[0] * tensor
    tiny_all = tiny_all.reshape((devices,) + tiny.shape)
    tokens_all = tokens_all.reshape(rows_all, width)
    cot_all = cot_all.reshape(rows_all, width)
    w_attn = w_attn[:, :rows_own].reshape(width, 4 * local_width)
    w_fc_all = w_fc_all[:, :rows_own].reshape(width, local_hidden)
    w_proj_all = w_proj_all[:, :rows_own].reshape(width, local_hidden)
    w_in, w_out_t = w_attn[:, : 3 * local_width], w_attn[:, 3 * local_width :]
    vectors = tiny_all[:, :8, :small].transpose(1, 0, 2).reshape(8, width)
    norm_gains, norm_shifts, qv_whole, res_whole = (
        vectors[0:2],
        vectors[2:4],
        vectors[4:6],
        vectors[6:8],
    )
    qv_local = lax.dynamic_slice_in_dim(qv_whole, head_start, local_width, 1)
    fc_local = lax.dynamic_slice_in_dim(tiny_all, place * dp, dp, 0)[
        :, 8 : 8 + fc_rows, :small
    ].reshape(local_hidden)

    xhat1_all, _ = standardize(tokens_all.astype(jnp.float32))
    ln1_all = (xhat1_all * norm_gains[0] + norm_shifts[0]).astype(half)
    residual_stream = tokens.astype(jnp.float32)
    first_standardized, first_inverse_deviation = standardize(residual_stream)
    qkv = jnp.dot(ln1_all, w_in, preferred_element_type=jnp.float32)
    bias3 = jnp.concatenate([qv_local[0], jnp.zeros_like(qv_local[0]), qv_local[1]])
    qkv = (qkv + bias3).astype(half)

    def split(array):
        return array.reshape(seqs, length, heads_local, HEAD_DIM)

    query, keys, value = (
        split(qkv[:, i * local_width : (i + 1) * local_width]) for i in range(3)
    )
    context, logsum = lax.map(attend, (query, keys, value, segments))
    context = context.reshape(rows_all, local_width)
    attn_part = contract_cols(context, w_out_t).astype(half)
    (attn_sum,) = exchange(
        dp, tensor, 2, [(LineSum, "tensor", attn_part.reshape(tensor, -1, width))]
    )
    first_hidden = residual_stream + attn_sum + res_whole[0]
    second_standardized, second_inverse_deviation = standardize(first_hidden)
    ln2 = (second_standardized * norm_gains[1] + norm_shifts[1]).astype(half)
    (ln2_all,) = exchange(dp, tensor, 3, [(LineGather, "tensor", ln2)])
    ln2_all = ln2_all.reshape(rows_all, width)
    pre = jnp.dot(ln2_all, w_fc_all, preferred_element_type=jnp.float32) + fc_local
    act = gelu_value(pre).astype(half)
    mlp_part = contract_cols(act, w_proj_all).astype(half)
    d_pre = jnp.dot(cot_all, w_proj_all, preferred_element_type=jnp.float32) * gelu_slope(pre)
    fcb_grad = jnp.sum(d_pre, axis=0)
    d_pre_half = d_pre.astype(half)
    d_ln2_part = contract_cols(d_pre_half, w_fc_all).astype(half)
    proj_grad = contract_rows(cot_all, act).astype(half)
    fc_grad = contract_rows(ln2_all, d_pre_half).astype(half)

    def blocks(array):
        return pad_to(array.reshape(dp, rows_own, array.shape[1]), 1, rows_pad)

    d_ln2, mlp_sum, proj_part, fc_part = exchange(
        dp,
        tensor,
        4,
        [
            (LineSum, "tensor", d_ln2_part.reshape(tensor, -1, width)),
            (LineSum, "tensor", mlp_part.reshape(tensor, -1, width)),
            (PairSum, "dp", blocks(proj_grad)),
            (PairSum, "dp", blocks(fc_grad)),
        ],
    )
    block_out = (first_hidden + mlp_sum + res_whole[1]).astype(half)
    residual_gradient = cotangent.astype(jnp.float32)
    res1_grad = jnp.sum(residual_gradient, axis=0)
    second_gain_gradient = jnp.sum(d_ln2 * second_standardized, axis=0)
    shift2_grad = jnp.sum(d_ln2, axis=0)
    first_hidden_gradient = residual_gradient + layer_normalize_backward(
        d_ln2, second_standardized, second_inverse_deviation, norm_gains[1]
    )
    res0_grad = jnp.sum(first_hidden_gradient, axis=0)
    (d_hidden_all,) = exchange(
        dp, tensor, 5, [(LineGather, "tensor", first_hidden_gradient.astype(half))]
    )
    d_hidden_all = d_hidden_all.reshape(rows_all, width)
    out_grad = contract_rows(d_hidden_all, context)
    d_context = jnp.dot(d_hidden_all, w_out_t, preferred_element_type=jnp.float32).astype(half)
    grads = lax.map(attend_back, (query, keys, value, segments, logsum, split(d_context)))
    grad_query, grad_key, grad_value = (grad.reshape(rows_all, local_width) for grad in grads)
    qb_grad = jnp.sum(grad_query, axis=0)
    vb_grad = jnp.sum(grad_value, axis=0)
    d_qkv = jnp.concatenate([grad_query, grad_key, grad_value], axis=1).astype(half)
    qkv_grad = contract_rows(ln1_all, d_qkv)
    attn_grad = jnp.concatenate([qkv_grad, out_grad], axis=1).astype(half)
    d_ln1_part = contract_cols(d_qkv, w_in)
    first_gain_gradient = jnp.sum(d_ln1_part * xhat1_all, axis=0)
    shift1_grad = jnp.sum(d_ln1_part, axis=0)

    qv_spread = lax.dynamic_update_slice(
        jnp.zeros((2, width), jnp.float32), jnp.stack([qb_grad, vb_grad]), (0, head_start)
    )
    fc_spread = lax.dynamic_update_slice(
        jnp.zeros((devices, fc_rows, small), jnp.float32),
        fcb_grad.reshape(dp, fc_rows, small),
        (place * dp, 0, 0),
    )
    vector_grads = jnp.stack(
        [
            first_gain_gradient,
            second_gain_gradient,
            shift1_grad,
            shift2_grad,
            qv_spread[0],
            qv_spread[1],
            res0_grad,
            res1_grad,
        ]
    )
    tiny_grads = jnp.concatenate(
        [vector_grads.reshape(8, devices, small).transpose(1, 0, 2), fc_spread], axis=1
    )
    tiny_grads = pad_to(pad_to(tiny_grads, 2, 128), 1, 16)
    tiny_grads = tiny_grads.reshape((dp, tensor) + tiny_grads.shape[1:])
    tiny_sum, d_ln1, attn_grad_part = exchange(
        dp,
        tensor,
        6,
        [
            (GridSum, "all", tiny_grads),
            (LineSum, "tensor", d_ln1_part.astype(half).reshape(tensor, -1, width)),
            (PairSum, "dp", blocks(attn_grad)),
        ],
    )
    block_input_gradient = (
        first_hidden_gradient
        + layer_normalize_backward(
            d_ln1, first_standardized, first_inverse_deviation, norm_gains[0]
        )
    ).astype(half)
    attn_grad_part = attn_grad_part[:rows_own]
    qkv_part = jnp.stack(
        [attn_grad_part[:, i * local_width : (i + 1) * local_width] for i in range(3)]
    )
    return (
        block_out,
        block_input_gradient,
        tiny_sum[0:2, :small],
        tiny_sum[2:4, :small],
        qkv_part,
        tiny_sum[4:6, :small],
        attn_grad_part[:, 3 * local_width :].T,
        tiny_sum[6:8, :small],
        fc_part[:rows_own],
        tiny_sum[8 : 8 + fc_rows, :small].reshape(fc_bias.shape[0]),
        proj_part[:rows_own].T,
    )


def solution(mesh):
    return jax.shard_map(
        functools.partial(shards, mesh.shape["dp"], mesh.shape["tensor"]),
        mesh=mesh,
        in_specs=(
            P(("dp", "tensor"), None),
            P(None, ("dp", "tensor")),
            P(None, ("dp", "tensor")),
            P(None, "dp", "tensor"),
            P(None, ("dp", "tensor")),
            P("tensor", "dp"),
            P(None, ("dp", "tensor")),
            P("dp", "tensor"),
            P(("dp", "tensor")),
            P("tensor", "dp"),
            P("dp", None),
            P(("dp", "tensor"), None),
        ),
        out_specs=(
            P(("dp", "tensor"), None),
            P(("dp", "tensor"), None),
            P(None, ("dp", "tensor")),
            P(None, ("dp", "tensor")),
            P(None, "dp", "tensor"),
            P(None, ("dp", "tensor")),
            P("tensor", "dp"),
            P(None, ("dp", "tensor")),
            P("dp", "tensor"),
            P(("dp", "tensor")),
            P("tensor", "dp"),
        ),
        check_vma=False,
    )
```

```python
import functools

import jax
import jax.numpy as jnp
from jax import lax
from jax.experimental import pallas as pl
from jax.experimental.pallas import tpu as pltpu
from jax.sharding import PartitionSpec as P

HEAD_DIM = 64


epsilon = 1e-05
gelu_coeff = 0.044715
gelu_root = 0.7978845608028654


def layer_normalize(rows, norm_gain, norm_shift):
    centered_input = rows - jnp.mean(rows, axis=-1, keepdims=True)
    inverse_deviation = lax.rsqrt(
        jnp.mean(centered_input * centered_input, axis=-1, keepdims=True) + epsilon
    )
    standardized_input = centered_input * inverse_deviation
    return (standardized_input * norm_gain + norm_shift, standardized_input, inverse_deviation)


def layer_normalize_backward(output_gradient, standardized_input, inverse_deviation, norm_gain):
    scaled_rows = output_gradient * norm_gain
    return inverse_deviation * (
        scaled_rows
        - jnp.mean(scaled_rows, axis=-1, keepdims=True)
        - standardized_input * jnp.mean(scaled_rows * standardized_input, axis=-1, keepdims=True)
    )


def gelu_value(pre):
    return 0.5 * pre * (1.0 + jnp.tanh(gelu_root * (pre + gelu_coeff * pre * pre * pre)))


def gelu_slope(pre):
    tangent = jnp.tanh(gelu_root * (pre + gelu_coeff * pre * pre * pre))
    return 0.5 * (1.0 + tangent) + 0.5 * pre * (1.0 - tangent * tangent) * gelu_root * (
        1.0 + 3.0 * gelu_coeff * pre * pre
    )


def allowed_pairs(segment):
    length = segment.shape[0]
    rows = lax.broadcasted_iota(jnp.int32, (length, length), 0)
    cols = lax.broadcasted_iota(jnp.int32, (length, length), 1)
    return (segment[:, None] == segment[None, :]) & (rows >= cols)


def masked_scores(query, key, segment):
    scores = jnp.einsum(
        "qhd,khd->hqk", query, key, preferred_element_type=jnp.float32
    ) * HEAD_DIM ** (-0.5)
    return jnp.where(allowed_pairs(segment)[None], scores, -1e30)


def attend(pieces):
    query, key, value, segment = pieces
    scores = masked_scores(query, key, segment)
    peak = jnp.max(scores, axis=-1, keepdims=True)
    logsum = peak + jnp.log(jnp.sum(jnp.exp(scores - peak), axis=-1, keepdims=True))
    weights = jnp.exp(scores - logsum).astype(jnp.bfloat16)
    context = jnp.einsum("hqk,khd->qhd", weights, value, preferred_element_type=jnp.float32)
    return (context.astype(jnp.bfloat16), logsum)


def attend_back(pieces):
    query, key, value, segment, logsum, grad_context = pieces
    probs = jnp.exp(masked_scores(query, key, segment) - logsum)
    probs_half = probs.astype(jnp.bfloat16)
    grad_value = jnp.einsum(
        "hqk,qhd->khd", probs_half, grad_context, preferred_element_type=jnp.float32
    )
    grad_probs = jnp.einsum("qhd,khd->hqk", grad_context, value, preferred_element_type=jnp.float32)
    inner = jnp.sum(probs * grad_probs, axis=-1, keepdims=True)
    grad_scores = (probs * (grad_probs - inner)).astype(jnp.bfloat16)
    grad_query = jnp.einsum(
        "hqk,khd->qhd", grad_scores, key, preferred_element_type=jnp.float32
    ) * HEAD_DIM ** (-0.5)
    grad_key = jnp.einsum(
        "hqk,qhd->khd", grad_scores, query, preferred_element_type=jnp.float32
    ) * HEAD_DIM ** (-0.5)
    return (grad_query, grad_key, grad_value)


def contract_rows(left, right):
    return lax.dot_general(
        left, right, (((0,), (0,)), ((), ())), preferred_element_type=jnp.float32
    )


def contract_cols(left, right):
    return lax.dot_general(
        left, right, (((1,), (1,)), ((), ())), preferred_element_type=jnp.float32
    )


MESH = pl.DeviceIdType.MESH


def loop(count, body):
    if count <= 8:
        for step in range(count):
            body(step)
    else:

        def wrapped(step, carry):
            body(step)
            return carry

        lax.fori_loop(0, count, wrapped, 0)


def remote(src, dst, send, recv, device):
    return pltpu.make_async_remote_copy(
        src_ref=src, dst_ref=dst, send_sem=send, recv_sem=recv, device_id=device, device_id_type=MESH
    )


class GridGather:
    def __init__(self, dp, tensor, d, t, src, out, sems, local_sem):
        self.dp, self.tensor, self.d, self.t = dp, tensor, d, t
        self.src, self.out, self.sems = src, out, sems
        self.local = pltpu.make_async_copy(src, out.at[d, t], local_sem)

    def first(self, step):
        k = step + 1
        return remote(
            self.src,
            self.out.at[self.d, self.t],
            self.sems.at[0, k],
            self.sems.at[1, k],
            {"dp": self.d, "tensor": lax.rem(self.t + k, self.tensor)},
        )

    def second(self, step):
        k = step + 1
        return remote(
            self.out.at[self.d],
            self.out.at[self.d],
            self.sems.at[2, k],
            self.sems.at[3, k],
            {"dp": lax.rem(self.d + k, self.dp), "tensor": self.t},
        )

    def start(self):
        self.local.start()
        loop(self.tensor - 1, lambda step: self.first(step).start())

    def middle(self):
        self.local.wait()
        loop(self.tensor - 1, lambda step: self.first(step).wait())
        loop(self.dp - 1, lambda step: self.second(step).start())

    def finish(self):
        loop(self.dp - 1, lambda step: self.second(step).wait())


class GridSum:
    def __init__(self, dp, tensor, d, t, src, out, sems, slots, sums):
        self.dp, self.tensor, self.d, self.t = dp, tensor, d, t
        self.src, self.out, self.sems = src, out, sems
        self.slots, self.sums = slots, sums

    def first(self, step):
        k = step + 1
        peer = lax.rem(self.d + k, self.dp)
        return remote(
            self.src.at[peer],
            self.slots.at[k],
            self.sems.at[0, k],
            self.sems.at[1, k],
            {"dp": peer, "tensor": self.t},
        )

    def second(self, step):
        k = step + 1
        peer = lax.rem(self.t + k, self.tensor)
        return remote(
            self.sums.at[0, peer],
            self.sums.at[1, k],
            self.sems.at[2, k],
            self.sems.at[3, k],
            {"dp": self.d, "tensor": peer},
        )

    def start(self):
        loop(self.dp - 1, lambda step: self.first(step).start())

    def middle(self):
        self.sums[0] = self.src[self.d]

        def add(step):
            self.first(step).wait()
            self.sums[0] += self.slots[step + 1]

        loop(self.dp - 1, add)
        loop(self.tensor - 1, lambda step: self.second(step).start())

    def finish(self):
        self.out[...] = self.sums[0, self.t]

        def add(step):
            self.second(step).wait()
            self.out[...] += self.sums[1, step + 1]

        loop(self.tensor - 1, add)


class LineGather:
    def __init__(self, n, me, device, src, out, sems, local_sem):
        self.n, self.me, self.device, self.src, self.out, self.sems = n, me, device, src, out, sems
        self.local = pltpu.make_async_copy(src, out.at[me], local_sem)

    def move(self, side, block, src=None):
        peer = lax.rem(self.me + (1 if side == 0 else self.n - 1), self.n)
        return remote(
            self.out.at[block] if src is None else src,
            self.out.at[block],
            self.sems.at[2 * side, block],
            self.sems.at[2 * side + 1, block],
            self.device(peer),
        )

    def start(self):
        @pl.when(self.me < self.n - 1)
        def _():
            self.move(0, self.me, self.src).start()

        @pl.when(self.me > 0)
        def _():
            self.move(1, self.me, self.src).start()

        self.local.start()

    def middle(self):
        for step in range(1, self.n):

            @pl.when(self.me >= step)
            def _():
                block = self.me - step
                self.move(0, block).wait_recv()

                @pl.when(self.me < self.n - 1)
                def _():
                    self.move(0, block).start()

            @pl.when(self.me + step < self.n)
            def _():
                block = self.me + step
                self.move(1, block).wait_recv()

                @pl.when(self.me > 0)
                def _():
                    self.move(1, block).start()

    def finish(self):
        for step in range(self.n):

            @pl.when((self.me >= step) & (self.me < self.n - 1))
            def _():
                self.move(0, self.me - step).wait_send()

            @pl.when((self.me + step < self.n) & (self.me > 0))
            def _():
                self.move(1, self.me + step).wait_send()

        self.local.wait()


class FlatSum:
    def __init__(self, n, me, device, src, out, sems, slots):
        self.n, self.me, self.device, self.src, self.out, self.sems = n, me, device, src, out, sems
        self.slots = slots

    def copy(self, step):
        k = step + 1
        peer = lax.rem(self.me + k, self.n)
        return remote(
            self.src.at[peer],
            self.slots.at[k],
            self.sems.at[0, k],
            self.sems.at[1, k],
            self.device(peer),
        )

    def start(self):
        loop(self.n - 1, lambda step: self.copy(step).start())

    def middle(self):
        pass

    def finish(self):
        self.out[...] = self.src[self.me].astype(jnp.float32)

        def add(step):
            self.copy(step).wait()
            self.out[...] += self.slots[step + 1].astype(jnp.float32)

        loop(self.n - 1, add)


class PairGather:
    def __init__(self, n, me, device, src, out, sems, local_sem):
        self.n, self.me, self.device, self.src, self.out, self.sems = n, me, device, src, out, sems
        self.chips, self.core = n // 2, lax.rem(me, 2)
        self.chip = me // 2
        self.sibling = self.chip * 2 + 1 - self.core
        self.local = pltpu.make_async_copy(src, out.at[me], local_sem)

    def across(self, step):
        k = step + 1
        peer = lax.rem(self.chip + k, self.chips) * 2 + self.core
        return remote(
            self.src,
            self.out.at[self.me],
            self.sems.at[0, k],
            self.sems.at[1, k],
            self.device(peer),
        )

    def to_sibling(self):
        return remote(
            self.src,
            self.out.at[self.me],
            self.sems.at[0, 0],
            self.sems.at[1, 0],
            self.device(self.sibling),
        )

    def hand(self, step):
        k = step + 1
        slot = lax.rem(self.chip + self.chips - k, self.chips) * 2 + self.core
        return remote(
            self.out.at[slot],
            self.out.at[slot],
            self.sems.at[2, k],
            self.sems.at[3, k],
            self.device(self.sibling),
        )

    def start(self):
        loop(self.chips - 1, lambda step: self.across(step).start())
        self.to_sibling().start()
        self.local.start()

    def middle(self):
        def step_through(step):
            self.across(step).wait_recv()
            self.hand(step).start()

        loop(self.chips - 1, step_through)

    def finish(self):
        loop(self.chips - 1, lambda step: self.across(step).wait_send())
        self.to_sibling().wait()
        loop(self.chips - 1, lambda step: self.hand(step).wait())
        self.local.wait()


class PairSum:
    def __init__(self, n, me, device, src, out, sems, slots, sums):
        self.n, self.me, self.device, self.src, self.out, self.sems = n, me, device, src, out, sems
        self.slots, self.sums = slots, sums
        self.chips, self.core = n // 2, lax.rem(me, 2)
        self.chip = me // 2
        self.sibling = self.chip * 2 + 1 - self.core

    def trade(self, step):
        target = lax.rem(self.chip + step + 1, self.chips)
        return remote(
            self.src.at[target * 2 + 1 - self.core],
            self.slots.at[step],
            self.sems.at[0, step],
            self.sems.at[1, step],
            self.device(self.sibling),
        )

    def across(self, step):
        target = lax.rem(self.chip + step + 1, self.chips)
        return remote(
            self.sums.at[step],
            self.slots.at[self.chips + step],
            self.sems.at[2, step],
            self.sems.at[3, step],
            self.device(target * 2 + self.core),
        )

    def start(self):
        loop(self.chips, lambda step: self.trade(step).start())

    def middle(self):
        def pair(step):
            target = lax.rem(self.chip + step + 1, self.chips)
            self.trade(step).wait_recv()
            return self.src[target * 2 + self.core].astype(jnp.float32) + self.slots[step].astype(
                jnp.float32
            )

        def forward(step):
            self.sums[step] = pair(step).astype(self.sums.dtype)
            self.across(step).start()

        loop(self.chips - 1, forward)
        self.out[...] = pair(self.chips - 1)

    def finish(self):
        loop(self.chips, lambda step: self.trade(step).wait_send())

        def add(step):
            self.across(step).wait()
            self.out[...] += self.slots[self.chips + step].astype(jnp.float32)

        loop(self.chips - 1, add)


def exchange(dp, tensor, identity, ops):
    sizes = {"dp": dp, "tensor": tensor, "all": dp * tensor}
    arrays = [array for _, _, array in ops]
    outs, scratch, counts = [], [], []
    for form, axis, array in ops:
        n = sizes[axis]
        mine = [pltpu.SemaphoreType.DMA((4, max(dp, tensor) if axis == "all" else n))]
        if form is GridGather:
            outs.append(jax.ShapeDtypeStruct((dp, tensor) + array.shape, array.dtype))
            mine.append(pltpu.SemaphoreType.DMA)
        elif form in (LineGather, PairGather):
            outs.append(jax.ShapeDtypeStruct((n,) + array.shape, array.dtype))
            mine.append(pltpu.SemaphoreType.DMA)
        elif form is GridSum:
            outs.append(jax.ShapeDtypeStruct(array.shape[2:], jnp.float32))
            mine.append(pltpu.VMEM(array.shape, array.dtype))
            mine.append(pltpu.VMEM((2,) + array.shape[1:], array.dtype))
        else:
            outs.append(jax.ShapeDtypeStruct(array.shape[1:], jnp.float32))
            mine.append(pltpu.VMEM(array.shape, array.dtype))
            if form is PairSum:
                mine.append(pltpu.VMEM((n // 2,) + array.shape[1:], array.dtype))
        scratch += mine
        counts.append(len(mine))
    axes = {axis for _, axis, _ in ops}
    if "all" in axes:
        axes = {"dp", "tensor"}

    def kernel(*refs):
        sources = refs[: len(ops)]
        results = refs[len(ops) : 2 * len(ops)]
        rest = list(refs[2 * len(ops) :])
        d, t = lax.axis_index("dp"), lax.axis_index("tensor")
        ranks = {"dp": d, "tensor": t}
        devices = {
            "dp": lambda i: {"dp": i, "tensor": t},
            "tensor": lambda i: {"dp": d, "tensor": i},
        }
        barrier = pltpu.get_barrier_semaphore()
        for axis in sorted(axes):
            n = sizes[axis]

            def greet(step, n=n, axis=axis):
                pl.semaphore_signal(
                    barrier,
                    inc=1,
                    device_id=devices[axis](lax.rem(ranks[axis] + step + 1, n)),
                    device_id_type=MESH,
                )

            loop(n - 1, greet)
        pl.semaphore_wait(barrier, sum(sizes[axis] - 1 for axis in axes))
        work = []
        for (form, axis, _), src, out, count in zip(ops, sources, results, counts):
            if axis == "all":
                work.append(form(dp, tensor, d, t, src, out, *rest[:count]))
            else:
                work.append(form(sizes[axis], ranks[axis], devices[axis], src, out, *rest[:count]))
            del rest[:count]
        for op in work:
            op.start()
        order = [GridGather, GridSum, PairSum, FlatSum, LineGather, PairGather]
        for op in sorted(work, key=lambda op: order.index(type(op))):
            op.middle()
        for op in work:
            op.finish()

    return pl.pallas_call(
        kernel,
        out_shape=tuple(outs),
        in_specs=[pl.BlockSpec(memory_space=pltpu.VMEM)] * len(ops),
        out_specs=tuple([pl.BlockSpec(memory_space=pltpu.VMEM)] * len(ops)),
        scratch_shapes=scratch,
        compiler_params=pltpu.CompilerParams(
            collective_id=identity, has_side_effects=True, vmem_limit_bytes=40 * 2**20
        ),
        name="exchange_%d" % identity,
    )(*arrays)


def pad_to(array, axis, size):
    widths = [(0, 0)] * array.ndim
    widths[axis] = (0, size - array.shape[axis])
    return jnp.pad(array, widths) if size > array.shape[axis] else array


def standardize(rows):
    centered = rows - jnp.mean(rows, axis=-1, keepdims=True)
    inverse = lax.rsqrt(jnp.mean(centered * centered, axis=-1, keepdims=True) + epsilon)
    return centered * inverse, inverse


def shards(
    dp,
    tensor,
    tokens,
    norm_gain_pair,
    norm_bias_pair,
    w_qkv,
    qv_bias,
    w_out,
    res_bias,
    w_fc,
    fc_bias,
    w_proj,
    segments,
    cotangent,
):
    place = lax.axis_index("tensor")
    devices = dp * tensor
    width = tokens.shape[1]
    rows_own = w_qkv.shape[1]
    rows_pad = -(-rows_own // 16) * 16
    local_width = w_qkv.shape[2]
    local_hidden = w_fc.shape[1]
    seqs, length = segments.shape
    heads_local = local_width // HEAD_DIM
    head_start = place * local_width
    hidden_start = place * local_hidden
    small = norm_gain_pair.shape[1]
    fc_rows = fc_bias.shape[0] // small
    half = jnp.bfloat16

    attention_weights = jnp.concatenate([w_qkv[0], w_qkv[1], w_qkv[2], w_out.T], axis=1)
    tiny = jnp.concatenate(
        [norm_gain_pair, norm_bias_pair, qv_bias, res_bias, fc_bias.reshape(fc_rows, small)], axis=0
    )
    tiny = pad_to(pad_to(tiny, 1, 128), 0, 16)
    tiny_all, tokens_all, w_attn = exchange(
        dp,
        tensor,
        1,
        [
            (GridGather, "all", tiny),
            (LineGather, "tensor", tokens),
            (PairGather, "dp", pad_to(attention_weights, 0, rows_pad)),
        ],
    )
    rows_all = tokens.shape[0] * tensor
    tiny_all = tiny_all.reshape((devices,) + tiny.shape)
    tokens_all = tokens_all.reshape(rows_all, width)
    w_attn = w_attn[:, :rows_own].reshape(width, 4 * local_width)
    w_in, w_out_t = w_attn[:, : 3 * local_width], w_attn[:, 3 * local_width :]
    vectors = tiny_all[:, :8, :small].transpose(1, 0, 2).reshape(8, width)
    norm_gains, norm_shifts, qv_whole, res_whole = (
        vectors[0:2],
        vectors[2:4],
        vectors[4:6],
        vectors[6:8],
    )
    qv_local = lax.dynamic_slice_in_dim(qv_whole, head_start, local_width, 1)
    fc_local = lax.dynamic_slice_in_dim(tiny_all, place * dp, dp, 0)[
        :, 8 : 8 + fc_rows, :small
    ].reshape(local_hidden)

    xhat1_all, _ = standardize(tokens_all.astype(jnp.float32))
    ln1_all = (xhat1_all * norm_gains[0] + norm_shifts[0]).astype(half)
    residual_stream = tokens.astype(jnp.float32)
    first_standardized, first_inverse_deviation = standardize(residual_stream)
    qkv = jnp.dot(ln1_all, w_in, preferred_element_type=jnp.float32)
    bias3 = jnp.concatenate([qv_local[0], jnp.zeros_like(qv_local[0]), qv_local[1]])
    qkv = (qkv + bias3).astype(half)

    def split(array):
        return array.reshape(seqs, length, heads_local, HEAD_DIM)

    query, keys, value = (
        split(qkv[:, i * local_width : (i + 1) * local_width]) for i in range(3)
    )
    context, logsum = lax.map(attend, (query, keys, value, segments))
    context = context.reshape(rows_all, local_width)
    attn_part = contract_cols(context, w_out_t).astype(half)
    attn_sum, cot_all, w_fc_all, w_proj_all = exchange(
        dp,
        tensor,
        2,
        [
            (FlatSum, "tensor", attn_part.reshape(tensor, -1, width)),
            (LineGather, "tensor", cotangent),
            (PairGather, "dp", pad_to(w_fc, 0, rows_pad)),
            (PairGather, "dp", pad_to(w_proj.T, 0, rows_pad)),
        ],
    )
    cot_all = cot_all.reshape(rows_all, width)
    w_fc_all = w_fc_all[:, :rows_own].reshape(width, local_hidden)
    w_proj_all = w_proj_all[:, :rows_own].reshape(width, local_hidden)
    first_hidden = residual_stream + attn_sum + res_whole[0]
    second_standardized, second_inverse_deviation = standardize(first_hidden)
    ln2 = (second_standardized * norm_gains[1] + norm_shifts[1]).astype(half)
    (ln2_all,) = exchange(dp, tensor, 3, [(LineGather, "tensor", ln2)])
    ln2_all = ln2_all.reshape(rows_all, width)
    pre = jnp.dot(ln2_all, w_fc_all, preferred_element_type=jnp.float32) + fc_local
    act = gelu_value(pre).astype(half)
    mlp_part = contract_cols(act, w_proj_all).astype(half)
    d_pre = jnp.dot(cot_all, w_proj_all, preferred_element_type=jnp.float32) * gelu_slope(pre)
    fcb_grad = jnp.sum(d_pre, axis=0)
    d_pre_half = d_pre.astype(half)
    d_ln2_part = contract_cols(d_pre_half, w_fc_all).astype(half)
    proj_grad = contract_rows(cot_all, act).astype(half)
    fc_grad = contract_rows(ln2_all, d_pre_half).astype(half)

    def blocks(array):
        return pad_to(array.reshape(dp, rows_own, array.shape[1]), 1, rows_pad)

    d_ln2, proj_part = exchange(
        dp,
        tensor,
        4,
        [
            (FlatSum, "tensor", d_ln2_part.reshape(tensor, -1, width)),
            (PairSum, "dp", blocks(proj_grad)),
        ],
    )
    residual_gradient = cotangent.astype(jnp.float32)
    res1_grad = jnp.sum(residual_gradient, axis=0)
    second_gain_gradient = jnp.sum(d_ln2 * second_standardized, axis=0)
    shift2_grad = jnp.sum(d_ln2, axis=0)
    first_hidden_gradient = residual_gradient + layer_normalize_backward(
        d_ln2, second_standardized, second_inverse_deviation, norm_gains[1]
    )
    res0_grad = jnp.sum(first_hidden_gradient, axis=0)
    d_hidden_all, mlp_sum, fc_part = exchange(
        dp,
        tensor,
        5,
        [
            (LineGather, "tensor", first_hidden_gradient.astype(half)),
            (FlatSum, "tensor", mlp_part.reshape(tensor, -1, width)),
            (PairSum, "dp", blocks(fc_grad)),
        ],
    )
    block_out = (first_hidden + mlp_sum + res_whole[1]).astype(half)
    d_hidden_all = d_hidden_all.reshape(rows_all, width)
    out_grad = contract_rows(d_hidden_all, context)
    d_context = jnp.dot(d_hidden_all, w_out_t, preferred_element_type=jnp.float32).astype(half)
    grads = lax.map(attend_back, (query, keys, value, segments, logsum, split(d_context)))
    grad_query, grad_key, grad_value = (grad.reshape(rows_all, local_width) for grad in grads)
    qb_grad = jnp.sum(grad_query, axis=0)
    vb_grad = jnp.sum(grad_value, axis=0)
    d_qkv = jnp.concatenate([grad_query, grad_key, grad_value], axis=1).astype(half)
    qkv_grad = contract_rows(ln1_all, d_qkv)
    attn_grad = jnp.concatenate([qkv_grad, out_grad], axis=1).astype(half)
    d_ln1_part = contract_cols(d_qkv, w_in)
    first_gain_gradient = jnp.sum(d_ln1_part * xhat1_all, axis=0)
    shift1_grad = jnp.sum(d_ln1_part, axis=0)

    qv_spread = lax.dynamic_update_slice(
        jnp.zeros((2, width), jnp.float32), jnp.stack([qb_grad, vb_grad]), (0, head_start)
    )
    fc_spread = lax.dynamic_update_slice(
        jnp.zeros((devices, fc_rows, small), jnp.float32),
        fcb_grad.reshape(dp, fc_rows, small),
        (place * dp, 0, 0),
    )
    vector_grads = jnp.stack(
        [
            first_gain_gradient,
            second_gain_gradient,
            shift1_grad,
            shift2_grad,
            qv_spread[0],
            qv_spread[1],
            res0_grad,
            res1_grad,
        ]
    )
    tiny_grads = jnp.concatenate(
        [vector_grads.reshape(8, devices, small).transpose(1, 0, 2), fc_spread], axis=1
    )
    tiny_grads = pad_to(pad_to(tiny_grads, 2, 128), 1, 16)
    tiny_grads = tiny_grads.reshape((dp, tensor) + tiny_grads.shape[1:])
    tiny_sum, d_ln1, attn_grad_part = exchange(
        dp,
        tensor,
        6,
        [
            (GridSum, "all", tiny_grads),
            (FlatSum, "tensor", d_ln1_part.astype(half).reshape(tensor, -1, width)),
            (PairSum, "dp", blocks(attn_grad)),
        ],
    )
    block_input_gradient = (
        first_hidden_gradient
        + layer_normalize_backward(
            d_ln1, first_standardized, first_inverse_deviation, norm_gains[0]
        )
    ).astype(half)
    attn_grad_part = attn_grad_part[:rows_own]
    qkv_part = jnp.stack(
        [attn_grad_part[:, i * local_width : (i + 1) * local_width] for i in range(3)]
    )
    return (
        block_out,
        block_input_gradient,
        tiny_sum[0:2, :small],
        tiny_sum[2:4, :small],
        qkv_part,
        tiny_sum[4:6, :small],
        attn_grad_part[:, 3 * local_width :].T,
        tiny_sum[6:8, :small],
        fc_part[:rows_own],
        tiny_sum[8 : 8 + fc_rows, :small].reshape(fc_bias.shape[0]),
        proj_part[:rows_own].T,
    )


def solution(mesh):
    return jax.shard_map(
        functools.partial(shards, mesh.shape["dp"], mesh.shape["tensor"]),
        mesh=mesh,
        in_specs=(
            P(("dp", "tensor"), None),
            P(None, ("dp", "tensor")),
            P(None, ("dp", "tensor")),
            P(None, "dp", "tensor"),
            P(None, ("dp", "tensor")),
            P("tensor", "dp"),
            P(None, ("dp", "tensor")),
            P("dp", "tensor"),
            P(("dp", "tensor")),
            P("tensor", "dp"),
            P("dp", None),
            P(("dp", "tensor"), None),
        ),
        out_specs=(
            P(("dp", "tensor"), None),
            P(("dp", "tensor"), None),
            P(None, ("dp", "tensor")),
            P(None, ("dp", "tensor")),
            P(None, "dp", "tensor"),
            P(None, ("dp", "tensor")),
            P("tensor", "dp"),
            P(None, ("dp", "tensor")),
            P("dp", "tensor"),
            P(("dp", "tensor")),
            P("tensor", "dp"),
        ),
        check_vma=False,
    )
```

```python
import functools

import jax
import jax.numpy as jnp
from jax import lax
from jax.experimental import pallas as pl
from jax.experimental.pallas import tpu as pltpu
from jax.sharding import PartitionSpec as P

HEAD_DIM = 64


epsilon = 1e-05
gelu_coeff = 0.044715
gelu_root = 0.7978845608028654


def layer_normalize(rows, norm_gain, norm_shift):
    centered_input = rows - jnp.mean(rows, axis=-1, keepdims=True)
    inverse_deviation = lax.rsqrt(
        jnp.mean(centered_input * centered_input, axis=-1, keepdims=True) + epsilon
    )
    standardized_input = centered_input * inverse_deviation
    return (standardized_input * norm_gain + norm_shift, standardized_input, inverse_deviation)


def layer_normalize_backward(output_gradient, standardized_input, inverse_deviation, norm_gain):
    scaled_rows = output_gradient * norm_gain
    return inverse_deviation * (
        scaled_rows
        - jnp.mean(scaled_rows, axis=-1, keepdims=True)
        - standardized_input * jnp.mean(scaled_rows * standardized_input, axis=-1, keepdims=True)
    )


def gelu_value(pre):
    return 0.5 * pre * (1.0 + jnp.tanh(gelu_root * (pre + gelu_coeff * pre * pre * pre)))


def gelu_slope(pre):
    tangent = jnp.tanh(gelu_root * (pre + gelu_coeff * pre * pre * pre))
    return 0.5 * (1.0 + tangent) + 0.5 * pre * (1.0 - tangent * tangent) * gelu_root * (
        1.0 + 3.0 * gelu_coeff * pre * pre
    )


def allowed_pairs(segment):
    length = segment.shape[0]
    rows = lax.broadcasted_iota(jnp.int32, (length, length), 0)
    cols = lax.broadcasted_iota(jnp.int32, (length, length), 1)
    return (segment[:, None] == segment[None, :]) & (rows >= cols)


def masked_scores(query, key, segment):
    scores = jnp.einsum(
        "qhd,khd->hqk", query, key, preferred_element_type=jnp.float32
    ) * HEAD_DIM ** (-0.5)
    return jnp.where(allowed_pairs(segment)[None], scores, -1e30)


def attend(pieces):
    query, key, value, segment = pieces
    scores = masked_scores(query, key, segment)
    peak = jnp.max(scores, axis=-1, keepdims=True)
    logsum = peak + jnp.log(jnp.sum(jnp.exp(scores - peak), axis=-1, keepdims=True))
    weights = jnp.exp(scores - logsum).astype(jnp.bfloat16)
    context = jnp.einsum("hqk,khd->qhd", weights, value, preferred_element_type=jnp.float32)
    return (context.astype(jnp.bfloat16), logsum)


def attend_back(pieces):
    query, key, value, segment, logsum, grad_context = pieces
    probs = jnp.exp(masked_scores(query, key, segment) - logsum)
    probs_half = probs.astype(jnp.bfloat16)
    grad_value = jnp.einsum(
        "hqk,qhd->khd", probs_half, grad_context, preferred_element_type=jnp.float32
    )
    grad_probs = jnp.einsum("qhd,khd->hqk", grad_context, value, preferred_element_type=jnp.float32)
    inner = jnp.sum(probs * grad_probs, axis=-1, keepdims=True)
    grad_scores = (probs * (grad_probs - inner)).astype(jnp.bfloat16)
    grad_query = jnp.einsum(
        "hqk,khd->qhd", grad_scores, key, preferred_element_type=jnp.float32
    ) * HEAD_DIM ** (-0.5)
    grad_key = jnp.einsum(
        "hqk,qhd->khd", grad_scores, query, preferred_element_type=jnp.float32
    ) * HEAD_DIM ** (-0.5)
    return (grad_query, grad_key, grad_value)


def contract_rows(left, right):
    return lax.dot_general(
        left, right, (((0,), (0,)), ((), ())), preferred_element_type=jnp.float32
    )


def contract_cols(left, right):
    return lax.dot_general(
        left, right, (((1,), (1,)), ((), ())), preferred_element_type=jnp.float32
    )


MESH = pl.DeviceIdType.MESH


def loop(count, body):
    if count <= 8:
        for step in range(count):
            body(step)
    else:

        def wrapped(step, carry):
            body(step)
            return carry

        lax.fori_loop(0, count, wrapped, 0)


def remote(src, dst, send, recv, device):
    return pltpu.make_async_remote_copy(
        src_ref=src, dst_ref=dst, send_sem=send, recv_sem=recv, device_id=device, device_id_type=MESH
    )


class GridGather:
    def __init__(self, dp, tensor, d, t, src, out, sems, local_sem):
        self.dp, self.tensor, self.d, self.t = dp, tensor, d, t
        self.src, self.out, self.sems = src, out, sems
        self.local = pltpu.make_async_copy(src, out.at[d, t], local_sem)

    def first(self, step):
        k = step + 1
        return remote(
            self.src,
            self.out.at[self.d, self.t],
            self.sems.at[0, k],
            self.sems.at[1, k],
            {"dp": self.d, "tensor": lax.rem(self.t + k, self.tensor)},
        )

    def second(self, step):
        k = step + 1
        return remote(
            self.out.at[self.d],
            self.out.at[self.d],
            self.sems.at[2, k],
            self.sems.at[3, k],
            {"dp": lax.rem(self.d + k, self.dp), "tensor": self.t},
        )

    def start(self):
        self.local.start()
        loop(self.tensor - 1, lambda step: self.first(step).start())

    def middle(self):
        self.local.wait()
        loop(self.tensor - 1, lambda step: self.first(step).wait())
        loop(self.dp - 1, lambda step: self.second(step).start())

    def finish(self):
        loop(self.dp - 1, lambda step: self.second(step).wait())


class GridSum:
    def __init__(self, dp, tensor, d, t, src, out, sems, slots, sums):
        self.dp, self.tensor, self.d, self.t = dp, tensor, d, t
        self.src, self.out, self.sems = src, out, sems
        self.slots, self.sums = slots, sums

    def first(self, step):
        k = step + 1
        peer = lax.rem(self.d + k, self.dp)
        return remote(
            self.src.at[peer],
            self.slots.at[k],
            self.sems.at[0, k],
            self.sems.at[1, k],
            {"dp": peer, "tensor": self.t},
        )

    def second(self, step):
        k = step + 1
        peer = lax.rem(self.t + k, self.tensor)
        return remote(
            self.sums.at[0, peer],
            self.sums.at[1, k],
            self.sems.at[2, k],
            self.sems.at[3, k],
            {"dp": self.d, "tensor": peer},
        )

    def start(self):
        loop(self.dp - 1, lambda step: self.first(step).start())

    def middle(self):
        self.sums[0] = self.src[self.d]

        def add(step):
            self.first(step).wait()
            self.sums[0] += self.slots[step + 1]

        loop(self.dp - 1, add)
        loop(self.tensor - 1, lambda step: self.second(step).start())

    def finish(self):
        self.out[...] = self.sums[0, self.t]

        def add(step):
            self.second(step).wait()
            self.out[...] += self.sums[1, step + 1]

        loop(self.tensor - 1, add)


class LineGather:
    def __init__(self, n, me, device, src, out, sems, local_sem):
        self.n, self.me, self.device, self.src, self.out, self.sems = n, me, device, src, out, sems
        self.local = pltpu.make_async_copy(src, out.at[me], local_sem)

    def move(self, side, block, src=None):
        peer = lax.rem(self.me + (1 if side == 0 else self.n - 1), self.n)
        return remote(
            self.out.at[block] if src is None else src,
            self.out.at[block],
            self.sems.at[2 * side, block],
            self.sems.at[2 * side + 1, block],
            self.device(peer),
        )

    def start(self):
        @pl.when(self.me < self.n - 1)
        def _():
            self.move(0, self.me, self.src).start()

        @pl.when(self.me > 0)
        def _():
            self.move(1, self.me, self.src).start()

        self.local.start()

    def middle(self):
        for step in range(1, self.n):

            @pl.when(self.me >= step)
            def _():
                block = self.me - step
                self.move(0, block).wait_recv()

                @pl.when(self.me < self.n - 1)
                def _():
                    self.move(0, block).start()

            @pl.when(self.me + step < self.n)
            def _():
                block = self.me + step
                self.move(1, block).wait_recv()

                @pl.when(self.me > 0)
                def _():
                    self.move(1, block).start()

    def finish(self):
        for step in range(self.n):

            @pl.when((self.me >= step) & (self.me < self.n - 1))
            def _():
                self.move(0, self.me - step).wait_send()

            @pl.when((self.me + step < self.n) & (self.me > 0))
            def _():
                self.move(1, self.me + step).wait_send()

        self.local.wait()


class FlatSum:
    def __init__(self, n, me, device, src, out, sems, slots):
        self.n, self.me, self.device, self.src, self.out, self.sems = n, me, device, src, out, sems
        self.slots = slots

    def copy(self, step):
        k = step + 1
        peer = lax.rem(self.me + k, self.n)
        return remote(
            self.src.at[peer],
            self.slots.at[k],
            self.sems.at[0, k],
            self.sems.at[1, k],
            self.device(peer),
        )

    def start(self):
        loop(self.n - 1, lambda step: self.copy(step).start())

    def middle(self):
        pass

    def finish(self):
        self.out[...] = self.src[self.me].astype(jnp.float32)

        def add(step):
            self.copy(step).wait()
            self.out[...] += self.slots[step + 1].astype(jnp.float32)

        loop(self.n - 1, add)


class PairGather:
    def __init__(self, n, me, device, src, out, sems, local_sem):
        self.n, self.me, self.device, self.src, self.out, self.sems = n, me, device, src, out, sems
        self.chips, self.core = n // 2, lax.rem(me, 2)
        self.chip = me // 2
        self.sibling = self.chip * 2 + 1 - self.core
        self.local = pltpu.make_async_copy(src, out.at[me], local_sem)

    def across(self, step):
        k = step + 1
        peer = lax.rem(self.chip + k, self.chips) * 2 + self.core
        return remote(
            self.src,
            self.out.at[self.me],
            self.sems.at[0, k],
            self.sems.at[1, k],
            self.device(peer),
        )

    def to_sibling(self):
        return remote(
            self.src,
            self.out.at[self.me],
            self.sems.at[0, 0],
            self.sems.at[1, 0],
            self.device(self.sibling),
        )

    def hand(self, step):
        k = step + 1
        slot = lax.rem(self.chip + self.chips - k, self.chips) * 2 + self.core
        return remote(
            self.out.at[slot],
            self.out.at[slot],
            self.sems.at[2, k],
            self.sems.at[3, k],
            self.device(self.sibling),
        )

    def start(self):
        loop(self.chips - 1, lambda step: self.across(step).start())
        self.to_sibling().start()
        self.local.start()

    def middle(self):
        def step_through(step):
            self.across(step).wait_recv()
            self.hand(step).start()

        loop(self.chips - 1, step_through)

    def finish(self):
        loop(self.chips - 1, lambda step: self.across(step).wait_send())
        self.to_sibling().wait()
        loop(self.chips - 1, lambda step: self.hand(step).wait())
        self.local.wait()


class PairSum:
    def __init__(self, n, me, device, src, out, sems, slots, sums):
        self.n, self.me, self.device, self.src, self.out, self.sems = n, me, device, src, out, sems
        self.slots, self.sums = slots, sums
        self.chips, self.core = n // 2, lax.rem(me, 2)
        self.chip = me // 2
        self.sibling = self.chip * 2 + 1 - self.core

    def trade(self, step):
        target = lax.rem(self.chip + step + 1, self.chips)
        return remote(
            self.src.at[target * 2 + 1 - self.core],
            self.slots.at[step],
            self.sems.at[0, step],
            self.sems.at[1, step],
            self.device(self.sibling),
        )

    def across(self, step):
        target = lax.rem(self.chip + step + 1, self.chips)
        return remote(
            self.sums.at[step],
            self.slots.at[self.chips + step],
            self.sems.at[2, step],
            self.sems.at[3, step],
            self.device(target * 2 + self.core),
        )

    def start(self):
        loop(self.chips, lambda step: self.trade(step).start())

    def middle(self):
        def pair(step):
            target = lax.rem(self.chip + step + 1, self.chips)
            self.trade(step).wait_recv()
            return self.src[target * 2 + self.core].astype(jnp.float32) + self.slots[step].astype(
                jnp.float32
            )

        def forward(step):
            self.sums[step] = pair(step).astype(self.sums.dtype)
            self.across(step).start()

        loop(self.chips - 1, forward)
        self.out[...] = pair(self.chips - 1)

    def finish(self):
        loop(self.chips, lambda step: self.trade(step).wait_send())

        def add(step):
            self.across(step).wait()
            self.out[...] += self.slots[self.chips + step].astype(jnp.float32)

        loop(self.chips - 1, add)


def exchange(dp, tensor, identity, ops):
    sizes = {"dp": dp, "tensor": tensor, "all": dp * tensor}
    arrays = [array for _, _, array in ops]
    outs, scratch, counts = [], [], []
    for form, axis, array in ops:
        n = sizes[axis]
        mine = [pltpu.SemaphoreType.DMA((4, max(dp, tensor) if axis == "all" else n))]
        if form is GridGather:
            outs.append(jax.ShapeDtypeStruct((dp, tensor) + array.shape, array.dtype))
            mine.append(pltpu.SemaphoreType.DMA)
        elif form in (LineGather, PairGather):
            outs.append(jax.ShapeDtypeStruct((n,) + array.shape, array.dtype))
            mine.append(pltpu.SemaphoreType.DMA)
        elif form is GridSum:
            outs.append(jax.ShapeDtypeStruct(array.shape[2:], jnp.float32))
            mine.append(pltpu.VMEM(array.shape, array.dtype))
            mine.append(pltpu.VMEM((2,) + array.shape[1:], array.dtype))
        else:
            outs.append(jax.ShapeDtypeStruct(array.shape[1:], jnp.float32))
            mine.append(pltpu.VMEM(array.shape, array.dtype))
            if form is PairSum:
                mine.append(pltpu.VMEM((n // 2,) + array.shape[1:], array.dtype))
        scratch += mine
        counts.append(len(mine))
    axes = {axis for _, axis, _ in ops}
    if "all" in axes:
        axes = {"dp", "tensor"}

    def kernel(*refs):
        sources = refs[: len(ops)]
        results = refs[len(ops) : 2 * len(ops)]
        rest = list(refs[2 * len(ops) :])
        d, t = lax.axis_index("dp"), lax.axis_index("tensor")
        ranks = {"dp": d, "tensor": t}
        devices = {
            "dp": lambda i: {"dp": i, "tensor": t},
            "tensor": lambda i: {"dp": d, "tensor": i},
        }
        barrier = pltpu.get_barrier_semaphore()
        for axis in sorted(axes):
            n = sizes[axis]

            def greet(step, n=n, axis=axis):
                pl.semaphore_signal(
                    barrier,
                    inc=1,
                    device_id=devices[axis](lax.rem(ranks[axis] + step + 1, n)),
                    device_id_type=MESH,
                )

            loop(n - 1, greet)
        pl.semaphore_wait(barrier, sum(sizes[axis] - 1 for axis in axes))
        work = []
        for (form, axis, _), src, out, count in zip(ops, sources, results, counts):
            if axis == "all":
                work.append(form(dp, tensor, d, t, src, out, *rest[:count]))
            else:
                work.append(form(sizes[axis], ranks[axis], devices[axis], src, out, *rest[:count]))
            del rest[:count]
        for op in work:
            op.start()
        order = [GridGather, GridSum, PairSum, FlatSum, LineGather, PairGather]
        for op in sorted(work, key=lambda op: order.index(type(op))):
            op.middle()
        for op in work:
            op.finish()

    return pl.pallas_call(
        kernel,
        out_shape=tuple(outs),
        in_specs=[pl.BlockSpec(memory_space=pltpu.VMEM)] * len(ops),
        out_specs=tuple([pl.BlockSpec(memory_space=pltpu.VMEM)] * len(ops)),
        scratch_shapes=scratch,
        compiler_params=pltpu.CompilerParams(
            collective_id=identity, has_side_effects=True, vmem_limit_bytes=40 * 2**20
        ),
        name="exchange_%d" % identity,
    )(*arrays)


def pad_to(array, axis, size):
    widths = [(0, 0)] * array.ndim
    widths[axis] = (0, size - array.shape[axis])
    return jnp.pad(array, widths) if size > array.shape[axis] else array


def standardize(rows):
    centered = rows - jnp.mean(rows, axis=-1, keepdims=True)
    inverse = lax.rsqrt(jnp.mean(centered * centered, axis=-1, keepdims=True) + epsilon)
    return centered * inverse, inverse


def shards(
    dp,
    tensor,
    tokens,
    norm_gain_pair,
    norm_bias_pair,
    w_qkv,
    qv_bias,
    w_out,
    res_bias,
    w_fc,
    fc_bias,
    w_proj,
    segments,
    cotangent,
):
    place = lax.axis_index("tensor")
    devices = dp * tensor
    width = tokens.shape[1]
    rows_own = w_qkv.shape[1]
    rows_pad = -(-rows_own // 16) * 16
    local_width = w_qkv.shape[2]
    local_hidden = w_fc.shape[1]
    seqs, length = segments.shape
    heads_local = local_width // HEAD_DIM
    head_start = place * local_width
    hidden_start = place * local_hidden
    small = norm_gain_pair.shape[1]
    fc_rows = fc_bias.shape[0] // small
    half = jnp.bfloat16

    attention_weights = jnp.concatenate([w_qkv[0], w_qkv[1], w_qkv[2], w_out.T], axis=1)
    tiny = jnp.concatenate(
        [norm_gain_pair, norm_bias_pair, qv_bias, res_bias, fc_bias.reshape(fc_rows, small)], axis=0
    )
    tiny = pad_to(pad_to(tiny, 1, 128), 0, 16)
    tiny_all, tokens_all, w_attn = exchange(
        dp,
        tensor,
        1,
        [
            (GridGather, "all", tiny),
            (LineGather, "tensor", tokens),
            (PairGather, "dp", pad_to(attention_weights, 0, rows_pad)),
        ],
    )
    rows_all = tokens.shape[0] * tensor
    tiny_all = tiny_all.reshape((devices,) + tiny.shape)
    tokens_all = tokens_all.reshape(rows_all, width)
    w_attn = w_attn[:, :rows_own].reshape(width, 4 * local_width)
    w_in, w_out_t = w_attn[:, : 3 * local_width], w_attn[:, 3 * local_width :]
    vectors = tiny_all[:, :8, :small].transpose(1, 0, 2).reshape(8, width)
    norm_gains, norm_shifts, qv_whole, res_whole = (
        vectors[0:2],
        vectors[2:4],
        vectors[4:6],
        vectors[6:8],
    )
    qv_local = lax.dynamic_slice_in_dim(qv_whole, head_start, local_width, 1)
    fc_local = lax.dynamic_slice_in_dim(tiny_all, place * dp, dp, 0)[
        :, 8 : 8 + fc_rows, :small
    ].reshape(local_hidden)

    xhat1_all, _ = standardize(tokens_all.astype(jnp.float32))
    ln1_all = (xhat1_all * norm_gains[0] + norm_shifts[0]).astype(half)
    residual_stream = tokens.astype(jnp.float32)
    first_standardized, first_inverse_deviation = standardize(residual_stream)
    qkv = jnp.dot(ln1_all, w_in, preferred_element_type=jnp.float32)
    bias3 = jnp.concatenate([qv_local[0], jnp.zeros_like(qv_local[0]), qv_local[1]])
    qkv = (qkv + bias3).astype(half)

    def split(array):
        return array.reshape(seqs, length, heads_local, HEAD_DIM)

    query, keys, value = (
        split(qkv[:, i * local_width : (i + 1) * local_width]) for i in range(3)
    )
    context, logsum = lax.map(attend, (query, keys, value, segments))
    context = context.reshape(rows_all, local_width)
    attn_part = contract_cols(context, w_out_t).astype(half)
    attn_sum, w_fc_all, w_proj_all = exchange(
        dp,
        tensor,
        2,
        [
            (FlatSum, "tensor", attn_part.reshape(tensor, -1, width)),
            (PairGather, "dp", pad_to(w_fc, 0, rows_pad)),
            (PairGather, "dp", pad_to(w_proj.T, 0, rows_pad)),
        ],
    )
    w_fc_all = w_fc_all[:, :rows_own].reshape(width, local_hidden)
    w_proj_all = w_proj_all[:, :rows_own].reshape(width, local_hidden)
    first_hidden = residual_stream + attn_sum + res_whole[0]
    second_standardized, second_inverse_deviation = standardize(first_hidden)
    ln2 = (second_standardized * norm_gains[1] + norm_shifts[1]).astype(half)
    ln2_all, cot_all = exchange(
        dp, tensor, 3, [(LineGather, "tensor", ln2), (LineGather, "tensor", cotangent)]
    )
    cot_all = cot_all.reshape(rows_all, width)
    ln2_all = ln2_all.reshape(rows_all, width)
    pre = jnp.dot(ln2_all, w_fc_all, preferred_element_type=jnp.float32) + fc_local
    act = gelu_value(pre).astype(half)
    mlp_part = contract_cols(act, w_proj_all).astype(half)
    d_pre = jnp.dot(cot_all, w_proj_all, preferred_element_type=jnp.float32) * gelu_slope(pre)
    fcb_grad = jnp.sum(d_pre, axis=0)
    d_pre_half = d_pre.astype(half)
    d_ln2_part = contract_cols(d_pre_half, w_fc_all).astype(half)
    proj_grad = contract_rows(cot_all, act).astype(half)
    fc_grad = contract_rows(ln2_all, d_pre_half).astype(half)

    def blocks(array):
        return pad_to(array.reshape(dp, rows_own, array.shape[1]), 1, rows_pad)

    d_ln2, proj_part = exchange(
        dp,
        tensor,
        4,
        [
            (FlatSum, "tensor", d_ln2_part.reshape(tensor, -1, width)),
            (PairSum, "dp", blocks(proj_grad)),
        ],
    )
    residual_gradient = cotangent.astype(jnp.float32)
    res1_grad = jnp.sum(residual_gradient, axis=0)
    second_gain_gradient = jnp.sum(d_ln2 * second_standardized, axis=0)
    shift2_grad = jnp.sum(d_ln2, axis=0)
    first_hidden_gradient = residual_gradient + layer_normalize_backward(
        d_ln2, second_standardized, second_inverse_deviation, norm_gains[1]
    )
    res0_grad = jnp.sum(first_hidden_gradient, axis=0)
    d_hidden_all, mlp_sum, fc_part = exchange(
        dp,
        tensor,
        5,
        [
            (LineGather, "tensor", first_hidden_gradient.astype(half)),
            (FlatSum, "tensor", mlp_part.reshape(tensor, -1, width)),
            (PairSum, "dp", blocks(fc_grad)),
        ],
    )
    block_out = (first_hidden + mlp_sum + res_whole[1]).astype(half)
    d_hidden_all = d_hidden_all.reshape(rows_all, width)
    out_grad = contract_rows(d_hidden_all, context)
    d_context = jnp.dot(d_hidden_all, w_out_t, preferred_element_type=jnp.float32).astype(half)
    grads = lax.map(attend_back, (query, keys, value, segments, logsum, split(d_context)))
    grad_query, grad_key, grad_value = (grad.reshape(rows_all, local_width) for grad in grads)
    qb_grad = jnp.sum(grad_query, axis=0)
    vb_grad = jnp.sum(grad_value, axis=0)
    d_qkv = jnp.concatenate([grad_query, grad_key, grad_value], axis=1).astype(half)
    qkv_grad = contract_rows(ln1_all, d_qkv)
    attn_grad = jnp.concatenate([qkv_grad, out_grad], axis=1).astype(half)
    d_ln1_part = contract_cols(d_qkv, w_in)
    first_gain_gradient = jnp.sum(d_ln1_part * xhat1_all, axis=0)
    shift1_grad = jnp.sum(d_ln1_part, axis=0)

    qv_spread = lax.dynamic_update_slice(
        jnp.zeros((2, width), jnp.float32), jnp.stack([qb_grad, vb_grad]), (0, head_start)
    )
    fc_spread = lax.dynamic_update_slice(
        jnp.zeros((devices, fc_rows, small), jnp.float32),
        fcb_grad.reshape(dp, fc_rows, small),
        (place * dp, 0, 0),
    )
    vector_grads = jnp.stack(
        [
            first_gain_gradient,
            second_gain_gradient,
            shift1_grad,
            shift2_grad,
            qv_spread[0],
            qv_spread[1],
            res0_grad,
            res1_grad,
        ]
    )
    tiny_grads = jnp.concatenate(
        [vector_grads.reshape(8, devices, small).transpose(1, 0, 2), fc_spread], axis=1
    )
    tiny_grads = pad_to(pad_to(tiny_grads, 2, 128), 1, 16)
    tiny_grads = tiny_grads.reshape((dp, tensor) + tiny_grads.shape[1:])
    tiny_sum, d_ln1, attn_grad_part = exchange(
        dp,
        tensor,
        6,
        [
            (GridSum, "all", tiny_grads),
            (FlatSum, "tensor", d_ln1_part.astype(half).reshape(tensor, -1, width)),
            (PairSum, "dp", blocks(attn_grad)),
        ],
    )
    block_input_gradient = (
        first_hidden_gradient
        + layer_normalize_backward(
            d_ln1, first_standardized, first_inverse_deviation, norm_gains[0]
        )
    ).astype(half)
    attn_grad_part = attn_grad_part[:rows_own]
    qkv_part = jnp.stack(
        [attn_grad_part[:, i * local_width : (i + 1) * local_width] for i in range(3)]
    )
    return (
        block_out,
        block_input_gradient,
        tiny_sum[0:2, :small],
        tiny_sum[2:4, :small],
        qkv_part,
        tiny_sum[4:6, :small],
        attn_grad_part[:, 3 * local_width :].T,
        tiny_sum[6:8, :small],
        fc_part[:rows_own],
        tiny_sum[8 : 8 + fc_rows, :small].reshape(fc_bias.shape[0]),
        proj_part[:rows_own].T,
    )


def solution(mesh):
    return jax.shard_map(
        functools.partial(shards, mesh.shape["dp"], mesh.shape["tensor"]),
        mesh=mesh,
        in_specs=(
            P(("dp", "tensor"), None),
            P(None, ("dp", "tensor")),
            P(None, ("dp", "tensor")),
            P(None, "dp", "tensor"),
            P(None, ("dp", "tensor")),
            P("tensor", "dp"),
            P(None, ("dp", "tensor")),
            P("dp", "tensor"),
            P(("dp", "tensor")),
            P("tensor", "dp"),
            P("dp", None),
            P(("dp", "tensor"), None),
        ),
        out_specs=(
            P(("dp", "tensor"), None),
            P(("dp", "tensor"), None),
            P(None, ("dp", "tensor")),
            P(None, ("dp", "tensor")),
            P(None, "dp", "tensor"),
            P(None, ("dp", "tensor")),
            P("tensor", "dp"),
            P(None, ("dp", "tensor")),
            P("dp", "tensor"),
            P(("dp", "tensor")),
            P("tensor", "dp"),
        ),
        check_vma=False,
    )
```
